32 devices in a mesh: beam: 8 (over y, x, core), seg: 4 (over z).
Axes of the slice: x: 2, y: 2, z: 4, core: 2. Of those that a mesh axis runs over, the one named last changes fastest.
Arguments:
- voltages: bfloat16 [2, 128, 4, 65536], P(None, 'beam', 'seg'), may hold values from -6 to 6
- surv_taps: bfloat16 [32], replicated, may hold values from -1 to 1
- ref_taps: bfloat16 [32], replicated, may hold values from -1 to 1
- tx_owner: int32 [4], replicated, may hold values from 0 to 127
- delay_start: int32 [4], replicated, may hold values from 0 to 384
- doppler_start: int32 [4], replicated, may hold values from 0 to 128
Outputs:
- maps: float32 [4, 128, 128, 128], P(None, 'beam', 'seg')
The draws below stay inside these ranges and needn't reach their ends.
All inputs are finite; a program needn't handle non-finite values.
Results may differ from the reference program's by a relative error of at most 0.0027.
Values may be sent and summed in bfloat16 or wider, within the bound.
No kernel may reach another device: no remote copies, remote signals or barrier semaphores. Data moves between devices by JAX's collectives and lax.ppermute only.
A program may use at most 128 MiB of HBM per device.

```python
import jax
import jax.numpy as jnp
from jax import lax

SEG_DEV = 1
TX = 4
DECIM = 4
TAPS = 32
BLOCK_LEN = 64
BLOCKS = 256
DELAYS = 128
DOPPLER = 128
MAXDELAY = 512
RAW = 65536
BEAMS = 128
SEGMENTS = 4
N_SEG = 4


def with_ends(drawn, rng, smallest, high):
    extent = drawn.shape
    spot = [jax.random.randint(jax.random.fold_in(rng, axis), (), 0, extent[axis]) for axis in range(len(extent))]
    drawn = drawn.at[tuple(spot)].set(smallest)
    longest = extent.index(max(extent))
    spot[longest] = (spot[longest] + 1) % extent[longest]
    return drawn.at[tuple(spot)].set(high)


def level_of(rng, dims, split, low, largest):
    loudness = 1.0
    for dim, shards_of in split:
        heights = jax.random.uniform(jax.random.fold_in(jax.random.fold_in(rng, 6), dim), (shards_of,), jnp.float32, low / len(split), largest / len(split))
        loudness = loudness * jnp.repeat(jnp.exp(heights), dims[dim] // shards_of).reshape((-1,) + (1,) * (len(dims) - 1 - dim))
    return loudness


def centred(own_key, shape, deviation, reach, pieces=(), held_as=jnp.bfloat16):
    result = deviation * jax.random.normal(own_key, shape, jnp.float32)
    if pieces:
        result = result * level_of(own_key, shape, pieces, -0.22, 0.18)
    return jnp.clip(result, -reach, reach).astype(held_as)


def setup_inputs(seed: int = 0) -> dict:
    streams_of = jax.random.split(jax.random.key(seed), 7)
    voltages = centred(streams_of[0], (2, BEAMS, SEGMENTS, RAW), 1.0, 6.0, ((1, 8), (2, 4)))
    surv_taps = centred(streams_of[1], (TAPS,), TAPS ** -0.5, 1.0)
    ref_taps = centred(streams_of[2], (TAPS,), TAPS ** -0.5, 1.0)
    tx_owner = with_ends(jax.random.randint(streams_of[3], (TX,), 0, BEAMS), jax.random.fold_in(streams_of[3], 1), 0, BEAMS - 1).astype(jnp.int32)
    delay_start = with_ends(jax.random.randint(streams_of[4], (TX,), 0, MAXDELAY - DELAYS + 1), jax.random.fold_in(streams_of[4], 1), 0, MAXDELAY - DELAYS).astype(jnp.int32)
    doppler_start = with_ends(jax.random.randint(streams_of[5], (TX,), 0, BLOCKS - DOPPLER + 1), jax.random.fold_in(streams_of[5], 1), 0, BLOCKS - DOPPLER).astype(jnp.int32)
    return dict(voltages=voltages, surv_taps=surv_taps, ref_taps=ref_taps, tx_owner=tx_owner, delay_start=delay_start, doppler_start=doppler_start)


def decimate(raw, taps):
    count = raw.shape[-1] // DECIM
    pads = [(0, 0)] * (raw.ndim - 1) + [(TAPS - 1, 0)]
    padded = jnp.pad(raw, pads)
    total = jnp.zeros(raw.shape[:-1] + (count,), jnp.float32)
    for tap in range(TAPS):
        begin = TAPS - 1 - tap
        piece = padded[..., begin:begin + DECIM * count:DECIM]
        total = total + taps[tap].astype(jnp.float32) * piece.astype(jnp.float32)
    return total.astype(jnp.bfloat16)


def segment_power(surv_seg, ref_seg, d_lo, cos_t, sin_t):
    beams = surv_seg.shape[1]
    span = BLOCK_LEN + DELAYS - 1
    extra = (DELAYS - 1 + BLOCK_LEN - 1) // BLOCK_LEN
    blocks_s = surv_seg.reshape(2, beams, BLOCKS, BLOCK_LEN).astype(jnp.float32)
    rpad = jnp.pad(ref_seg, ((0, 0), (MAXDELAY, extra * BLOCK_LEN)))
    start = (MAXDELAY - (DELAYS - 1) - d_lo).astype(jnp.int32)
    rwin = lax.dynamic_slice_in_dim(rpad, start, (BLOCKS + extra) * BLOCK_LEN, 1)
    rwin = rwin.reshape(2, BLOCKS + extra, BLOCK_LEN)
    window = jnp.concatenate([rwin[:, e:e + BLOCKS] for e in range(extra + 1)], axis=2)[..., :span]
    tiled = jnp.tile(window, (1, 1, BLOCK_LEN + 1))[..., :BLOCK_LEN * (span + 1)]
    toeplitz = tiled.reshape(2, BLOCKS, BLOCK_LEN, span + 1)[..., :DELAYS].astype(jnp.float32)
    scale = BLOCK_LEN ** -0.5
    s_re, s_im = blocks_s[0], blocks_s[1]
    u_re, u_im = toeplitz[0], toeplitz[1]
    c_re = (jnp.einsum("blm,lmi->bli", s_re, u_re) + jnp.einsum("blm,lmi->bli", s_im, u_im)) * scale
    c_im = (jnp.einsum("blm,lmi->bli", s_im, u_re) - jnp.einsum("blm,lmi->bli", s_re, u_im)) * scale
    c_re = c_re[..., ::-1].astype(jnp.bfloat16).astype(jnp.float32)
    c_im = c_im[..., ::-1].astype(jnp.bfloat16).astype(jnp.float32)
    cos_f = cos_t.astype(jnp.float32)
    sin_f = sin_t.astype(jnp.float32)
    x_re = jnp.einsum("blj,lf->bjf", c_re, cos_f) + jnp.einsum("blj,lf->bjf", c_im, sin_f)
    x_im = jnp.einsum("blj,lf->bjf", c_im, cos_f) - jnp.einsum("blj,lf->bjf", c_re, sin_f)
    return (x_re * x_re + x_im * x_im) * (1.0 / (4 * BLOCKS))


def tables(f_lo):
    ells = jnp.arange(BLOCKS, dtype=jnp.int32)
    freqs = f_lo.astype(jnp.int32) + jnp.arange(DOPPLER, dtype=jnp.int32) - BLOCKS // 2
    phase = (ells[:, None] * freqs[None, :]) % BLOCKS
    angle = (2.0 * jnp.pi / BLOCKS) * phase.astype(jnp.float32)
    return jnp.cos(angle).astype(jnp.bfloat16), jnp.sin(angle).astype(jnp.bfloat16)


def reference(voltages, surv_taps, ref_taps, tx_owner, delay_start, doppler_start):
    surv = decimate(voltages, surv_taps)

    def slot_map(trans):
        raw_ref = lax.dynamic_index_in_dim(voltages, tx_owner[trans].astype(jnp.int32), 1, keepdims=False)
        ref = decimate(raw_ref, ref_taps)
        d_lo = delay_start[trans]
        cos_t, sin_t = tables(doppler_start[trans])

        def group(total, index):
            for inner in range(SEG_DEV):
                seg = (index * SEG_DEV + inner).astype(jnp.int32)
                surv_seg = lax.dynamic_index_in_dim(surv, seg, 2, keepdims=False)
                ref_seg = lax.dynamic_index_in_dim(ref, seg, 1, keepdims=False)
                total = total + segment_power(surv_seg, ref_seg, d_lo, cos_t, sin_t)
            return total, None

        total, _ = lax.scan(group, jnp.zeros((BEAMS, DELAYS, DOPPLER), jnp.float32), jnp.arange(N_SEG, dtype=jnp.int32))
        return total / SEGMENTS

    return lax.map(slot_map, jnp.arange(TX, dtype=jnp.int32))
```

```python
import functools

import jax
import jax.numpy as jnp
import ml_dtypes
import numpy as np
from jax import lax
from jax.experimental import pallas as pl
from jax.experimental.pallas import tpu as pltpu
from jax.sharding import PartitionSpec as P

TX = 4
DECIM = 4
TAPS = 32
BLOCK_LEN = 64
BLOCKS = 256
DELAYS = 128
DOPPLER = 128
FFT = 256
STRIDE = DECIM * BLOCK_LEN
LEAD = 128
REACH = LEAD + STRIDE
GROUPS = 4
VMEM_LIMIT = 50 * 1024 * 1024


def split_bf16(table):
    hi = table.astype(ml_dtypes.bfloat16)
    lo = (table - hi.astype(np.float64)).astype(ml_dtypes.bfloat16)
    return hi, lo


def fourier(samples):
    angle = 2 * np.pi / FFT * (np.outer(np.arange(FFT), samples) % FFT)
    cos, sin = np.cos(angle), np.sin(angle)
    return np.block([[cos, sin], [-sin, cos]])


def surv_fourier():
    hi, lo = split_bf16(fourier(np.arange(BLOCK_LEN)))
    return np.concatenate([hi, lo], axis=1)


def ref_fourier():
    parts = [fourier(np.arange(BLOCK_LEN) + BLOCK_LEN * e) for e in range(4)]
    hi, lo = split_bf16(np.concatenate(parts, axis=1))
    return np.concatenate([hi, lo], axis=1)


def lag_table():
    lags = 191 - np.arange(192)
    angle = 2 * np.pi / FFT * (np.outer(lags, np.arange(FFT)) % FFT)
    cos, sin = np.cos(angle), np.sin(angle)
    scale = 1.0 / (FFT * np.sqrt(BLOCK_LEN))
    both = np.stack([np.concatenate([cos, sin], 1), np.concatenate([-sin, cos], 1)])
    return (both.astype(ml_dtypes.bfloat16).astype(np.float64) * scale).astype(
        ml_dtypes.bfloat16
    )


def doppler_tables(f_lo):
    ells = jnp.arange(BLOCKS, dtype=jnp.int32)
    freqs = f_lo + jnp.arange(DOPPLER, dtype=jnp.int32) - BLOCKS // 2
    phase = ells[:, None] * freqs[None, :] % BLOCKS
    angle = 2.0 * jnp.pi / BLOCKS * phase.astype(jnp.float32)
    cos = jnp.cos(angle).astype(jnp.bfloat16)
    sin = jnp.sin(angle).astype(jnp.bfloat16)
    return jnp.concatenate(
        [jnp.concatenate([cos, -sin], 1), jnp.concatenate([sin, cos], 1)], 0
    )


def nt_dot(left, right):
    return lax.dot_general(
        left, right, (((1,), (1,)), ((), ())), preferred_element_type=jnp.float32
    )


def decimate_kernel(
    beams, rows, local_ref, mine_ref, taps_ref, prev_ref, x_ref, s_ref, r_ref, band, keep_s, keep_r
):
    step = pl.program_id(0)

    @pl.when(step == 0)
    def _():
        shape = (REACH, 2 * BLOCK_LEN)
        q = lax.broadcasted_iota(jnp.int32, shape, 0)
        lane = lax.broadcasted_iota(jnp.int32, shape, 1)
        tap = LEAD + DECIM * (lane % BLOCK_LEN) - q
        first = lane < BLOCK_LEN
        both = jnp.zeros(shape, jnp.float32)
        for t in range(TAPS):
            value = jnp.where(first, taps_ref[0, t], taps_ref[1, t])
            both = jnp.where(tap == t, value, both)
        turned = pltpu.roll(both, BLOCK_LEN, 1)
        zero = jnp.zeros(shape, jnp.float32)
        half = 2 * BLOCK_LEN
        band[:REACH, :half] = jnp.where(first, both, zero).astype(jnp.bfloat16)
        band[REACH:, :half] = jnp.where(first, zero, turned).astype(jnp.bfloat16)
        band[:REACH, half:] = jnp.where(first, turned, zero).astype(jnp.bfloat16)
        band[REACH:, half:] = jnp.where(first, zero, both).astype(jnp.bfloat16)

    prev = prev_ref[...] * (step > 0).astype(jnp.bfloat16)
    x = jnp.concatenate([prev, x_ref[...]], axis=2)
    parts = []
    for c in range(2):
        parts.append(
            jnp.concatenate([x[c, :, l * STRIDE : l * STRIDE + REACH] for l in range(rows)], axis=0)
        )
    lhs = jnp.concatenate(parts, axis=1)
    out = jnp.dot(lhs, band[...], preferred_element_type=jnp.float32)
    keep_s[...] = out[:, : 2 * BLOCK_LEN]
    keep_r[...] = out[:, 2 * BLOCK_LEN :]
    for b in range(beams):
        s_ref[b] = keep_s[pl.ds(b, rows, stride=beams), :].astype(jnp.bfloat16)
    for k in range(TX):
        picked = keep_r[pl.ds(local_ref[k], rows, stride=beams), :]
        r_ref[k] = jnp.where(mine_ref[k] > 0, picked, 0.0).astype(jnp.bfloat16)


def decimate(volts, taps, local, mine):
    beams, raw = volts.shape[1:]
    rows = 32
    steps = raw // (rows * STRIDE)
    wide = rows * STRIDE
    blocks = raw // STRIDE
    return pl.pallas_call(
        functools.partial(decimate_kernel, beams, rows),
        grid=(steps,),
        in_specs=[
            pl.BlockSpec(memory_space=pltpu.SMEM),
            pl.BlockSpec(memory_space=pltpu.SMEM),
            pl.BlockSpec(memory_space=pltpu.SMEM),
            pl.BlockSpec(
                (2, beams, LEAD), lambda i: (0, 0, jnp.maximum(i * (wide // LEAD) - 1, 0))
            ),
            pl.BlockSpec((2, beams, wide), lambda i: (0, 0, i)),
        ],
        out_specs=[
            pl.BlockSpec((beams, rows, 2 * BLOCK_LEN), lambda i: (0, i, 0)),
            pl.BlockSpec((TX, rows, 2 * BLOCK_LEN), lambda i: (0, i, 0)),
        ],
        out_shape=[
            jax.ShapeDtypeStruct((beams, blocks, 2 * BLOCK_LEN), jnp.bfloat16),
            jax.ShapeDtypeStruct((TX, blocks, 2 * BLOCK_LEN), jnp.bfloat16),
        ],
        scratch_shapes=[
            pltpu.VMEM((2 * REACH, 4 * BLOCK_LEN), jnp.bfloat16),
            pltpu.VMEM((rows * beams, 2 * BLOCK_LEN), jnp.float32),
            pltpu.VMEM((rows * beams, 2 * BLOCK_LEN), jnp.float32),
        ],
        compiler_params=pltpu.CompilerParams(vmem_limit_bytes=VMEM_LIMIT),
        name="decimate",
    )(local, mine, taps, volts, volts)


PAD = 8


def spectra_kernel(shift_ref, table_ref, r_ref, out_ref, padded):
    k = pl.program_id(0)
    padded[:PAD] = jnp.zeros((PAD, 2 * BLOCK_LEN), jnp.float32)
    padded[PAD + BLOCKS :] = jnp.zeros((PAD, 2 * BLOCK_LEN), jnp.float32)
    padded[PAD : PAD + BLOCKS] = r_ref[0].astype(jnp.float32)
    start = PAD - 1 - shift_ref[k]
    window = jnp.concatenate(
        [padded[pl.ds(start + e, BLOCKS), :].astype(jnp.bfloat16) for e in range(4)], axis=1
    )
    both = jnp.concatenate([window, window], axis=1)
    out_ref[0] = nt_dot(table_ref[...], both)


def ref_spectra(shift, ref):
    table = jnp.asarray(ref_fourier())
    return pl.pallas_call(
        spectra_kernel,
        grid=(TX,),
        in_specs=[
            pl.BlockSpec(memory_space=pltpu.SMEM),
            pl.BlockSpec(table.shape, lambda k: (0, 0)),
            pl.BlockSpec((1, BLOCKS, 2 * BLOCK_LEN), lambda k: (k, 0, 0)),
        ],
        out_specs=pl.BlockSpec((1, 2 * FFT, BLOCKS), lambda k: (k, 0, 0)),
        out_shape=jax.ShapeDtypeStruct((TX, 2 * FFT, BLOCKS), jnp.float32),
        scratch_shapes=[pltpu.VMEM((BLOCKS + 2 * PAD, 2 * BLOCK_LEN), jnp.float32)],
        compiler_params=pltpu.CompilerParams(vmem_limit_bytes=VMEM_LIMIT),
        name="ref_spectra",
    )(shift, table, ref)


def power_kernel(chunks, table_ref, s_ref, r_ref, lag_ref, dop_ref, out_ref):
    s = s_ref[0]
    spec = nt_dot(table_ref[...], jnp.concatenate([s, s], axis=1))
    s_re, s_im = spec[:FFT], spec[FFT:]
    each = DELAYS // chunks
    for k in range(TX):
        r_re, r_im = r_ref[k, :FFT], r_ref[k, FFT:]
        p_re = (s_re * r_re + s_im * r_im).astype(jnp.bfloat16)
        p_im = (s_im * r_re - s_re * r_im).astype(jnp.bfloat16)
        prod = jnp.concatenate([p_re, p_im], axis=0)
        corr = jnp.dot(lag_ref[k], prod, preferred_element_type=jnp.float32)
        corr = corr.astype(jnp.bfloat16)
        corr = jnp.concatenate([corr[:DELAYS], corr[DELAYS:]], axis=1)
        x = jnp.dot(corr, dop_ref[k], preferred_element_type=jnp.float32)
        x_re, x_im = x[:, :DOPPLER], x[:, DOPPLER:]
        power = (x_re * x_re + x_im * x_im) * (1.0 / (4 * BLOCKS))
        for g in range(chunks):
            out_ref[g, k, 0] = power[g * each : (g + 1) * each].astype(jnp.bfloat16)


def powers(surv, first, count, spectra, lags, dops, chunks):
    table = jnp.asarray(surv_fourier())
    each = DELAYS // chunks
    return pl.pallas_call(
        functools.partial(power_kernel, chunks),
        grid=(count,),
        in_specs=[
            pl.BlockSpec(table.shape, lambda b: (0, 0)),
            pl.BlockSpec((1, BLOCKS, 2 * BLOCK_LEN), lambda b: (first + b, 0, 0)),
            pl.BlockSpec(spectra.shape, lambda b: (0, 0, 0)),
            pl.BlockSpec(lags.shape, lambda b: (0, 0, 0)),
            pl.BlockSpec(dops.shape, lambda b: (0, 0, 0)),
        ],
        out_specs=pl.BlockSpec((chunks, TX, 1, each, DOPPLER), lambda b: (0, 0, b, 0, 0)),
        out_shape=jax.ShapeDtypeStruct((chunks, TX, count, each, DOPPLER), jnp.bfloat16),
        compiler_params=pltpu.CompilerParams(vmem_limit_bytes=VMEM_LIMIT),
        cost_estimate=pl.CostEstimate(
            flops=count * TX * 2 * 768 * 65536, bytes_accessed=6 << 20, transcendentals=0
        ),
        name="powers",
    )(table, surv, spectra, lags, dops)


def shards(voltages, surv_taps, ref_taps, tx_owner, delay_start, doppler_start):
    beams_here = voltages.shape[1]
    n_beam = lax.axis_size("beam")
    n_seg = lax.axis_size("seg")
    me = lax.axis_index("beam")
    seg = lax.axis_index("seg")
    segments_all = n_seg * voltages.shape[2]
    volts = voltages.reshape(2, beams_here, voltages.shape[3])
    taps = jnp.stack([surv_taps, ref_taps]).astype(jnp.float32)
    mine = (tx_owner // beams_here == me).astype(jnp.int32)
    surv, ref = decimate(volts, taps, tx_owner % beams_here, mine)
    hop = 1
    while hop < n_beam:
        ref = ref + lax.ppermute(ref, "beam", [(i, i ^ hop) for i in range(n_beam)])
        hop *= 2
    lead = delay_start + (DELAYS - 1)
    spectra = ref_spectra(lead // BLOCK_LEN, ref)
    table = jnp.asarray(lag_table())
    lags = jnp.stack(
        [
            lax.dynamic_slice_in_dim(table, lead[k] % BLOCK_LEN, DELAYS, 1).reshape(
                2 * DELAYS, 2 * FFT
            )
            for k in range(TX)
        ]
    )
    dops = jnp.stack([doppler_tables(doppler_start[k]) for k in range(TX)])
    count = beams_here // GROUPS
    maps = []
    for g in range(GROUPS):
        part = powers(surv, g * count, count, spectra, lags, dops, n_seg)
        total = lax.dynamic_index_in_dim(part, seg, 0, keepdims=False).astype(jnp.float32)
        for turn in range(1, n_seg):
            send = lax.dynamic_index_in_dim(part, (seg + turn) % n_seg, 0, keepdims=False)
            got = lax.ppermute(send, "seg", [(i, (i + turn) % n_seg) for i in range(n_seg)])
            total = total + got.astype(jnp.float32)
        maps.append(total / segments_all)
    return jnp.concatenate(maps, axis=1)


def solution(mesh):
    return jax.shard_map(
        shards,
        mesh=mesh,
        in_specs=(P(None, "beam", "seg", None), P(), P(), P(), P(), P()),
        out_specs=P(None, "beam", "seg", None),
        check_vma=False,
    )
```

```python
import functools

import jax
import jax.numpy as jnp
import ml_dtypes
import numpy as np
from jax import lax
from jax.experimental import pallas as pl
from jax.experimental.pallas import tpu as pltpu
from jax.sharding import PartitionSpec as P

TX = 4
HALF_TX = TX // 2
DECIM = 4
TAPS = 32
BLOCK_LEN = 64
BLOCKS = 256
DELAYS = 128
DOPPLER = 128
FFT = 256
STRIDE = DECIM * BLOCK_LEN
LEAD = 128
REACH = LEAD + STRIDE
PAIR = 2 * BLOCK_LEN
GROUPS = 4
LANES = 128
LANE_BLOCKS = 2 * FFT // LANES
HALF_DELAYS = DELAYS // 2
VMEM_LIMIT = 24 * 1024 * 1024

SMEM = pl.BlockSpec(memory_space=pltpu.SMEM)
VMEM = pl.BlockSpec(memory_space=pltpu.VMEM)


def split_bf16(table):
    hi = table.astype(ml_dtypes.bfloat16)
    lo = (table - hi.astype(np.float64)).astype(ml_dtypes.bfloat16)
    return hi, lo


def fourier(samples):
    angle = 2 * np.pi / FFT * (np.outer(np.arange(FFT), samples) % FFT)
    cos, sin = np.cos(angle), np.sin(angle)
    return np.block([[cos, sin], [-sin, cos]])


def surv_fourier():
    hi, lo = split_bf16(fourier(np.arange(BLOCK_LEN)))
    return np.concatenate([hi, lo], axis=1)


def ref_fourier():
    parts = [fourier(np.arange(BLOCK_LEN) + BLOCK_LEN * e) for e in range(4)]
    hi, lo = split_bf16(np.concatenate(parts, axis=1))
    return np.concatenate([hi, lo], axis=1)


def in_lane_blocks(both):
    parts, rows, _ = both.shape
    return both.astype(np.float32).reshape(parts, rows, LANE_BLOCKS, LANES).swapaxes(1, 2)


def lag_table():
    lags = 191 - np.arange(192)
    angle = 2 * np.pi / FFT * (np.outer(lags, np.arange(FFT)) % FFT)
    cos, sin = np.cos(angle), np.sin(angle)
    scale = 1.0 / (FFT * np.sqrt(BLOCK_LEN))
    both = np.stack([np.concatenate([cos, sin], 1), np.concatenate([-sin, cos], 1)])
    both = both.astype(ml_dtypes.bfloat16).astype(np.float64) * scale
    return in_lane_blocks(both)


def doppler_table():
    freqs = np.arange(BLOCKS) - BLOCKS // 2
    angle = 2 * np.pi / BLOCKS * (np.outer(freqs, np.arange(BLOCKS)) % BLOCKS)
    cos, sin = np.cos(angle), np.sin(angle)
    both = np.stack([np.concatenate([cos, sin], 1), np.concatenate([-sin, cos], 1)])
    return in_lane_blocks(both.astype(ml_dtypes.bfloat16))


def nt_dot(left, right):
    return lax.dot_general(
        left, right, (((1,), (1,)), ((), ())), preferred_element_type=jnp.float32
    )


def dot(left, right):
    return jnp.dot(left, right, preferred_element_type=jnp.float32)


def decimate_kernel(beams, rows, ids, owner, staps, rtaps, prev_ref, x_ref, *refs):
    s_refs, (keep_ref, send_ref, band, all_s, all_r) = refs[:GROUPS], refs[GROUPS:]
    step = pl.program_id(0)

    @pl.when(step == 0)
    def _():
        shape = (REACH, PAIR)
        q = lax.broadcasted_iota(jnp.int32, shape, 0)
        lane = lax.broadcasted_iota(jnp.int32, shape, 1)
        tap = LEAD + DECIM * (lane % BLOCK_LEN) - q
        first = lane < BLOCK_LEN
        one, two = staps[...].astype(jnp.float32), rtaps[...].astype(jnp.float32)
        both = jnp.zeros(shape, jnp.float32)
        for t in range(TAPS):
            row = jnp.where(first[:1], one[:, t : t + 1], two[:, t : t + 1])
            both = jnp.where(tap == t, row, both)
        turned = pltpu.roll(both, BLOCK_LEN, 1)
        zero = jnp.zeros(shape, jnp.float32)
        band[:REACH, :PAIR] = jnp.where(first, both, zero).astype(jnp.bfloat16)
        band[REACH:, :PAIR] = jnp.where(first, zero, turned).astype(jnp.bfloat16)
        band[:REACH, PAIR:] = jnp.where(first, turned, zero).astype(jnp.bfloat16)
        band[REACH:, PAIR:] = jnp.where(first, zero, both).astype(jnp.bfloat16)

    prev = prev_ref[...] * (step > 0).astype(jnp.bfloat16)
    x = jnp.concatenate([prev, x_ref[...]], axis=2)
    parts = []
    for c in range(2):
        parts.append(
            jnp.concatenate([x[c, :, l * STRIDE : l * STRIDE + REACH] for l in range(rows)], axis=0)
        )
    out = dot(jnp.concatenate(parts, axis=1), band[...])
    all_s[...] = out[:, :PAIR]
    all_r[...] = out[:, PAIR:]
    count = beams // GROUPS
    for b in range(beams):
        picked = all_s[pl.ds(b, rows, stride=beams), :]
        s_refs[b // count][b % count] = picked.astype(jnp.bfloat16)
    core = ids[0] % 2
    for ref, first_tx in ((keep_ref, core * HALF_TX), (send_ref, (1 - core) * HALF_TX)):
        for k in range(HALF_TX):
            beam = owner[first_tx + k]
            picked = all_r[pl.ds(beam % beams, rows, stride=beams), :]
            ref[k] = jnp.where(beam // beams == ids[0], picked, 0.0).astype(jnp.bfloat16)


def decimate(volts, staps, rtaps, ids, owner):
    beams, raw = volts.shape[1:]
    rows = 64
    wide = rows * STRIDE
    blocks = raw // STRIDE
    count = beams // GROUPS
    block = lambda n: pl.BlockSpec((n, rows, PAIR), lambda i: (0, i, 0))
    shape = lambda n: jax.ShapeDtypeStruct((n, blocks, PAIR), jnp.bfloat16)
    return pl.pallas_call(
        functools.partial(decimate_kernel, beams, rows),
        grid=(raw // wide,),
        in_specs=[
            SMEM,
            SMEM,
            pl.BlockSpec((1, TAPS), lambda i: (0, 0)),
            pl.BlockSpec((1, TAPS), lambda i: (0, 0)),
            pl.BlockSpec(
                (2, beams, LEAD), lambda i: (0, 0, jnp.maximum(i * (wide // LEAD) - 1, 0))
            ),
            pl.BlockSpec((2, beams, wide), lambda i: (0, 0, i)),
        ],
        out_specs=[block(count)] * GROUPS + [block(HALF_TX)] * 2,
        out_shape=[shape(count)] * GROUPS + [shape(HALF_TX)] * 2,
        scratch_shapes=[
            pltpu.VMEM((2 * REACH, 2 * PAIR), jnp.bfloat16),
            pltpu.VMEM((rows * beams, PAIR), jnp.float32),
            pltpu.VMEM((rows * beams, PAIR), jnp.float32),
        ],
        compiler_params=pltpu.CompilerParams(vmem_limit_bytes=VMEM_LIMIT),
        name="decimate",
    )(ids, owner, staps, rtaps, volts, volts)


def tables_kernel(chunks, ids, delay, doppler, lag_ref, dop_ref, lags, dops):
    each = DELAYS // chunks
    for k in range(TX):
        base = (delay[k] + DELAYS - 1) % BLOCK_LEN
        for part in range(2):
            for n in range(chunks // 2):
                chunk = ids[1] ^ (2 * n)
                at = part * HALF_DELAYS + n * each
                for q in range(LANE_BLOCKS):
                    picked = lag_ref[part, q, pl.ds(base + chunk * each, each), :]
                    lags[k, at : at + each, q * LANES : (q + 1) * LANES] = picked.astype(jnp.bfloat16)
            for q in range(LANE_BLOCKS):
                picked = dop_ref[part, q, pl.ds(doppler[k], DOPPLER), :].T.astype(jnp.bfloat16)
                dops[k, q * LANES : (q + 1) * LANES, part * DOPPLER : (part + 1) * DOPPLER] = picked


def make_tables(ids, delay, doppler, chunks):
    return pl.pallas_call(
        functools.partial(tables_kernel, chunks),
        in_specs=[SMEM, SMEM, SMEM, VMEM, VMEM],
        out_specs=[VMEM, VMEM],
        out_shape=[
            jax.ShapeDtypeStruct((TX, DELAYS, 2 * FFT), jnp.bfloat16),
            jax.ShapeDtypeStruct((TX, 2 * BLOCKS, 2 * DOPPLER), jnp.bfloat16),
        ],
        compiler_params=pltpu.CompilerParams(vmem_limit_bytes=VMEM_LIMIT),
        name="tables",
    )(ids, delay, doppler, jnp.asarray(lag_table()), jnp.asarray(doppler_table()))


PAD = 8


def spectra_kernel(ids, delay, table_ref, mine_ref, other_ref, out_ref, padded):
    core = ids[0] % 2
    padded[:PAD] = jnp.zeros((PAD, PAIR), jnp.float32)
    padded[PAD + BLOCKS :] = jnp.zeros((PAD, PAIR), jnp.float32)
    for k in range(TX):
        here = core == k // HALF_TX
        ref = jnp.where(here, mine_ref[k % HALF_TX], other_ref[k % HALF_TX])
        padded[PAD : PAD + BLOCKS] = ref.astype(jnp.float32)
        start = PAD - 1 - (delay[k] + DELAYS - 1) // BLOCK_LEN
        window = jnp.concatenate(
            [padded[pl.ds(start + e, BLOCKS), :].astype(jnp.bfloat16) for e in range(4)], axis=1
        )
        out_ref[k] = nt_dot(table_ref[...], jnp.concatenate([window, window], axis=1))


def ref_spectra(ids, delay, mine, other):
    return pl.pallas_call(
        spectra_kernel,
        in_specs=[SMEM, SMEM, VMEM, VMEM, VMEM],
        out_specs=VMEM,
        out_shape=jax.ShapeDtypeStruct((TX, 2 * FFT, BLOCKS), jnp.float32),
        scratch_shapes=[pltpu.VMEM((BLOCKS + 2 * PAD, PAIR), jnp.float32)],
        compiler_params=pltpu.CompilerParams(vmem_limit_bytes=VMEM_LIMIT),
        name="ref_spectra",
    )(ids, delay, jnp.asarray(ref_fourier()), mine, other)


def power_kernel(
    chunks, table_ref, here_ref, there_ref, r_here, r_there, lag_ref, dop_ref, own_ref, send_ref, spec, prods, corrs
):
    count = here_ref.shape[0]
    each = DELAYS // chunks
    for n, ref in enumerate((here_ref, there_ref)):
        s = ref[...].reshape(count * BLOCKS, PAIR)
        spec[n] = nt_dot(table_ref[...], jnp.concatenate([s, s], axis=1))
    for k in range(TX):
        for n, r_ref in enumerate((r_here, r_there)):
            r_re, r_im = r_ref[k, :FFT], r_ref[k, FFT:]
            prod, corr = prods.at[n], corrs.at[k % 2]
            for b in range(count):
                cols = slice(b * BLOCKS, (b + 1) * BLOCKS)
                s_re, s_im = spec[n, :FFT, cols], spec[n, FFT:, cols]
                prod[:FFT, cols] = (s_re * r_re + s_im * r_im).astype(jnp.bfloat16)
                prod[FFT:, cols] = (s_im * r_re - s_re * r_im).astype(jnp.bfloat16)
            out = dot(lag_ref[k], prod[...]).astype(jnp.bfloat16)
            for b in range(count):
                cols = slice(b * BLOCKS, (b + 1) * BLOCKS)
                rows = slice((n * count + b) * HALF_DELAYS, (n * count + b + 1) * HALF_DELAYS)
                corr[rows, :BLOCKS] = out[:HALF_DELAYS, cols]
                corr[rows, BLOCKS:] = out[HALF_DELAYS:, cols]
        x = dot(corrs[k % 2], dop_ref[k])
        x_re, x_im = x[:, :DOPPLER], x[:, DOPPLER:]
        power = (x_re * x_re + x_im * x_im) * (1.0 / (4 * BLOCKS))
        power = power[: count * HALF_DELAYS] + power[count * HALF_DELAYS :]
        power = power.reshape(count, HALF_DELAYS, DOPPLER)
        own_ref[k] = power[:, :each]
        for n in range(1, chunks // 2):
            send_ref[n - 1, k] = power[:, n * each : (n + 1) * each].astype(jnp.bfloat16)


def powers(here, there, r_here, r_there, lags, dops, chunks):
    count = here.shape[0]
    each = DELAYS // chunks
    return pl.pallas_call(
        functools.partial(power_kernel, chunks),
        in_specs=[VMEM] * 7,
        out_specs=[VMEM] * 2,
        out_shape=[
            jax.ShapeDtypeStruct((TX, count, each, DOPPLER), jnp.float32),
            jax.ShapeDtypeStruct((chunks // 2 - 1, TX, count, each, DOPPLER), jnp.bfloat16),
        ],
        scratch_shapes=[
            pltpu.VMEM((2, 2 * FFT, count * BLOCKS), jnp.float32),
            pltpu.VMEM((2, 2 * FFT, count * BLOCKS), jnp.bfloat16),
            pltpu.VMEM((2, 2 * count * HALF_DELAYS, 2 * BLOCKS), jnp.bfloat16),
        ],
        compiler_params=pltpu.CompilerParams(vmem_limit_bytes=VMEM_LIMIT),
        cost_estimate=pl.CostEstimate(
            flops=2 * count * TX * 4 * 768 * 65536, bytes_accessed=6 << 20, transcendentals=0
        ),
        name="powers",
    )(jnp.asarray(surv_fourier()), here, there, r_here, r_there, lags, dops)


def swap(value, axis, flip):
    size = lax.axis_size(axis)
    return lax.ppermute(value, axis, [(i, i ^ flip) for i in range(size)])


def shards(voltages, surv_taps, ref_taps, tx_owner, delay_start, doppler_start):
    beams_here = voltages.shape[1]
    n_beam = lax.axis_size("beam")
    n_seg = lax.axis_size("seg")
    segments_all = n_seg * voltages.shape[2]
    ids = jnp.stack([lax.axis_index("beam"), lax.axis_index("seg")]).astype(jnp.int32)
    volts = voltages.reshape(2, beams_here, voltages.shape[3])
    out = decimate(volts, surv_taps.reshape(1, TAPS), ref_taps.reshape(1, TAPS), ids, tx_owner)
    surv, (keep, send) = out[:GROUPS], out[GROUPS:]
    half = keep + swap(send, "beam", 1)
    half, surv, ids = lax.optimization_barrier((half, surv, ids))
    got = [swap(half, "beam", flip) for flip in range(2, n_beam, 2)]
    there = [swap(s, "seg", 1) for s in surv]
    lags, dops = make_tables(ids, delay_start, doppler_start, n_seg)
    half = functools.reduce(jnp.add, got, half)
    far = swap(half, "seg", 1)
    r_here = ref_spectra(ids, delay_start, half, swap(half, "beam", 1))
    r_there = ref_spectra(ids, delay_start, far, swap(far, "beam", 1))
    maps = []
    for g in range(GROUPS):
        total, outgoing = powers(surv[g], there[g], r_here, r_there, lags, dops, n_seg)
        for n in range(1, n_seg // 2):
            total = total + swap(outgoing[n - 1], "seg", 2 * n).astype(jnp.float32)
        maps.append(total / segments_all)
    return jnp.concatenate(maps, axis=1)


def solution(mesh):
    return jax.shard_map(
        shards,
        mesh=mesh,
        in_specs=(P(None, "beam", "seg", None), P(), P(), P(), P(), P()),
        out_specs=P(None, "beam", "seg", None),
        check_vma=False,
    )
```

```python
import functools

import jax
import jax.numpy as jnp
import ml_dtypes
import numpy as np
from jax import lax
from jax.experimental import pallas as pl
from jax.experimental.pallas import tpu as pltpu
from jax.sharding import PartitionSpec as P

TX = 4
HALF_TX = TX // 2
DECIM = 4
TAPS = 32
BLOCK_LEN = 64
BLOCKS = 256
DELAYS = 128
DOPPLER = 128
FFT = 256
STRIDE = DECIM * BLOCK_LEN
LEAD = 128
REACH = LEAD + STRIDE
PAIR = 2 * BLOCK_LEN
GROUPS = 4
LANES = 128
LANE_BLOCKS = 2 * FFT // LANES
HALF_DELAYS = DELAYS // 2
VMEM_LIMIT = 24 * 1024 * 1024

SMEM = pl.BlockSpec(memory_space=pltpu.SMEM)
VMEM = pl.BlockSpec(memory_space=pltpu.VMEM)
HBM = pl.BlockSpec(memory_space=pltpu.HBM)


def split_bf16(table):
    hi = table.astype(ml_dtypes.bfloat16)
    lo = (table - hi.astype(np.float64)).astype(ml_dtypes.bfloat16)
    return hi, lo


def fourier(samples):
    angle = 2 * np.pi / FFT * (np.outer(np.arange(FFT), samples) % FFT)
    cos, sin = np.cos(angle), np.sin(angle)
    return np.block([[cos, sin], [-sin, cos]])


def surv_fourier():
    hi, lo = split_bf16(fourier(np.arange(BLOCK_LEN)))
    return np.concatenate([hi, lo], axis=1)


def ref_fourier():
    parts = [fourier(np.arange(BLOCK_LEN) + BLOCK_LEN * e) for e in range(4)]
    hi, lo = split_bf16(np.concatenate(parts, axis=1))
    return np.concatenate([hi, lo], axis=1)


def in_lane_blocks(both):
    parts, rows, _ = both.shape
    return both.astype(np.float32).reshape(parts, rows, LANE_BLOCKS, LANES).swapaxes(1, 2)


def lag_table():
    lags = 191 - np.arange(192)
    angle = 2 * np.pi / FFT * (np.outer(lags, np.arange(FFT)) % FFT)
    cos, sin = np.cos(angle), np.sin(angle)
    scale = 1.0 / (FFT * np.sqrt(BLOCK_LEN))
    both = np.stack([np.concatenate([cos, sin], 1), np.concatenate([-sin, cos], 1)])
    both = both.astype(ml_dtypes.bfloat16).astype(np.float64) * scale
    return in_lane_blocks(both)


def doppler_table():
    freqs = np.arange(BLOCKS) - BLOCKS // 2
    angle = 2 * np.pi / BLOCKS * (np.outer(freqs, np.arange(BLOCKS)) % BLOCKS)
    cos, sin = np.cos(angle), np.sin(angle)
    both = np.stack([np.concatenate([cos, sin], 1), np.concatenate([-sin, cos], 1)])
    return in_lane_blocks(both.astype(ml_dtypes.bfloat16))


def nt_dot(left, right):
    return lax.dot_general(
        left, right, (((1,), (1,)), ((), ())), preferred_element_type=jnp.float32
    )


def dot(left, right):
    return jnp.dot(left, right, preferred_element_type=jnp.float32)


def decimate_kernel(beams, ids, owner, delay, doppler, staps, rtaps, volts, *refs):
    s_refs, refs = refs[:GROUPS], refs[GROUPS:]
    keep_ref, send_ref, params, x, taps, small, band, all_s, all_r, sems, small_sems = refs
    chunks = sems.shape[0]
    raw = volts.shape[2]
    wide = raw // chunks
    rows = wide // STRIDE
    blocks = raw // STRIDE
    smalls = [
        pltpu.make_async_copy(ref, small.at[n], small_sems.at[n])
        for n, ref in enumerate((owner, delay, doppler))
    ]
    smalls += [
        pltpu.make_async_copy(ref, taps.at[n], small_sems.at[3 + n])
        for n, ref in enumerate((staps, rtaps))
    ]
    copies = [
        pltpu.make_async_copy(
            volts.at[:, :, pl.ds(n * wide, wide)],
            x.at[:, :, pl.ds(LEAD + n * wide, wide)],
            sems.at[n],
        )
        for n in range(chunks)
    ]
    for copy in smalls + copies:
        copy.start()
    x[:, :, :LEAD] = jnp.zeros((2, beams, LEAD), jnp.bfloat16)
    for copy in smalls:
        copy.wait()

    shape = (REACH, PAIR)
    q = lax.broadcasted_iota(jnp.int32, shape, 0)
    lane = lax.broadcasted_iota(jnp.int32, shape, 1)
    tap = LEAD + DECIM * (lane % BLOCK_LEN) - q
    first = lane < BLOCK_LEN
    one, two = taps[0].astype(jnp.float32), taps[1].astype(jnp.float32)
    both = jnp.zeros(shape, jnp.float32)
    for t in range(TAPS):
        row = jnp.where(first[:1], one[:, t : t + 1], two[:, t : t + 1])
        both = jnp.where(tap == t, row, both)
    turned = pltpu.roll(both, BLOCK_LEN, 1)
    zero = jnp.zeros(shape, jnp.float32)
    band[:REACH, :PAIR] = jnp.where(first, both, zero).astype(jnp.bfloat16)
    band[REACH:, :PAIR] = jnp.where(first, zero, turned).astype(jnp.bfloat16)
    band[:REACH, PAIR:] = jnp.where(first, turned, zero).astype(jnp.bfloat16)
    band[REACH:, PAIR:] = jnp.where(first, zero, both).astype(jnp.bfloat16)
    for k in range(TX):
        params[k] = small[1, k]
        params[TX + k] = small[2, k]
    params[2 * TX] = ids[0]
    params[2 * TX + 1] = ids[1]

    for n in range(chunks):
        copies[n].wait()
        parts = []
        for c in range(2):
            parts.append(
                jnp.concatenate(
                    [x[c, :, l * STRIDE : l * STRIDE + REACH] for l in range(n * rows, (n + 1) * rows)],
                    axis=0,
                )
            )
        out = dot(jnp.concatenate(parts, axis=1), band[...])
        span = slice(n * rows * beams, (n + 1) * rows * beams)
        all_s[span] = out[:, :PAIR]
        all_r[span] = out[:, PAIR:]
    core = ids[0] % 2
    for ref, first_tx in ((keep_ref, core * HALF_TX), (send_ref, (1 - core) * HALF_TX)):
        for k in range(HALF_TX):
            beam = small[0, first_tx + k]
            picked = all_r[pl.ds(beam % beams, blocks, stride=beams), :]
            ref[k] = jnp.where(beam // beams == ids[0], picked, 0.0).astype(jnp.bfloat16)
    count = beams // GROUPS
    for b in range(beams):
        picked = all_s[pl.ds(b, blocks, stride=beams), :]
        s_refs[b // count][b % count] = picked.astype(jnp.bfloat16)


def decimate(volts, staps, rtaps, ids, owner, delay, doppler):
    beams, raw = volts.shape[1:]
    blocks = raw // STRIDE
    count = beams // GROUPS
    chunks = 4
    arrays = (owner, delay, doppler, staps, rtaps, volts)
    shape = lambda n: jax.ShapeDtypeStruct((n, blocks, PAIR), jnp.bfloat16)
    return pl.pallas_call(
        functools.partial(decimate_kernel, beams),
        in_specs=[SMEM] + [HBM] * 6,
        out_specs=[VMEM] * (GROUPS + 2) + [SMEM],
        out_shape=[shape(count)] * GROUPS
        + [shape(HALF_TX)] * 2
        + [jax.ShapeDtypeStruct((2 * TX + 2,), jnp.int32)],
        scratch_shapes=[
            pltpu.VMEM((2, beams, LEAD + raw), jnp.bfloat16),
            pltpu.VMEM((2, 1, TAPS), jnp.bfloat16),
            pltpu.SMEM((3, TX), jnp.int32),
            pltpu.VMEM((2 * REACH, 2 * PAIR), jnp.bfloat16),
            pltpu.VMEM((blocks * beams, PAIR), jnp.float32),
            pltpu.VMEM((blocks * beams, PAIR), jnp.float32),
            pltpu.SemaphoreType.DMA((chunks,)),
            pltpu.SemaphoreType.DMA((5,)),
        ],
        compiler_params=pltpu.CompilerParams(vmem_limit_bytes=VMEM_LIMIT),
        name="decimate",
    )(ids, *(pltpu.with_memory_space_constraint(a, pltpu.HBM) for a in arrays))


def tables_kernel(chunks, params, lag_ref, dop_ref, lags, dops):
    each = DELAYS // chunks
    for k in range(TX):
        base = (params[k] + DELAYS - 1) % BLOCK_LEN
        for part in range(2):
            for n in range(chunks // 2):
                chunk = params[2 * TX + 1] ^ (2 * n)
                at = part * HALF_DELAYS + n * each
                for q in range(LANE_BLOCKS):
                    picked = lag_ref[part, q, pl.ds(base + chunk * each, each), :]
                    lags[k, at : at + each, q * LANES : (q + 1) * LANES] = picked.astype(jnp.bfloat16)
            for q in range(LANE_BLOCKS):
                picked = dop_ref[part, q, pl.ds(params[TX + k], DOPPLER), :].T.astype(jnp.bfloat16)
                dops[k, q * LANES : (q + 1) * LANES, part * DOPPLER : (part + 1) * DOPPLER] = picked


def make_tables(params, chunks):
    return pl.pallas_call(
        functools.partial(tables_kernel, chunks),
        in_specs=[SMEM, VMEM, VMEM],
        out_specs=[VMEM, VMEM],
        out_shape=[
            jax.ShapeDtypeStruct((TX, DELAYS, 2 * FFT), jnp.bfloat16),
            jax.ShapeDtypeStruct((TX, 2 * BLOCKS, 2 * DOPPLER), jnp.bfloat16),
        ],
        compiler_params=pltpu.CompilerParams(vmem_limit_bytes=VMEM_LIMIT),
        name="tables",
    )(params, jnp.asarray(lag_table()), jnp.asarray(doppler_table()))


PAD = 8


def write_ref_spectra(params, table_ref, mine_ref, other_ref, out_ref, padded):
    core = params[2 * TX] % 2
    padded[:PAD] = jnp.zeros((PAD, PAIR), jnp.float32)
    padded[PAD + BLOCKS :] = jnp.zeros((PAD, PAIR), jnp.float32)
    for k in range(TX):
        here = core == k // HALF_TX
        ref = jnp.where(here, mine_ref[k % HALF_TX], other_ref[k % HALF_TX])
        padded[PAD : PAD + BLOCKS] = ref.astype(jnp.float32)
        start = PAD - 1 - (params[k] + DELAYS - 1) // BLOCK_LEN
        window = jnp.concatenate(
            [padded[pl.ds(start + e, BLOCKS), :].astype(jnp.bfloat16) for e in range(4)], axis=1
        )
        out_ref[k] = nt_dot(table_ref[...], jnp.concatenate([window, window], axis=1))


def sum_powers(table_ref, segments, lag_ref, dop_ref, spec, prods, corrs, emit):
    count = segments[0][0].shape[0]
    rows = count * HALF_DELAYS
    for n, (s_ref, _) in enumerate(segments):
        s = s_ref[...].reshape(count * BLOCKS, PAIR)
        spec[n] = nt_dot(table_ref[...], jnp.concatenate([s, s], axis=1))
    for k in range(TX):
        corr = corrs.at[k % 2]
        for n, (_, r_ref) in enumerate(segments):
            r_re, r_im = r_ref[k, :FFT], r_ref[k, FFT:]
            prod = prods.at[n]
            for b in range(count):
                cols = slice(b * BLOCKS, (b + 1) * BLOCKS)
                s_re, s_im = spec[n, :FFT, cols], spec[n, FFT:, cols]
                prod[:FFT, cols] = (s_re * r_re + s_im * r_im).astype(jnp.bfloat16)
                prod[FFT:, cols] = (s_im * r_re - s_re * r_im).astype(jnp.bfloat16)
            out = dot(lag_ref[k], prod[...]).astype(jnp.bfloat16)
            for b in range(count):
                cols = slice(b * BLOCKS, (b + 1) * BLOCKS)
                at = n * rows + b * HALF_DELAYS
                corr[at : at + HALF_DELAYS, :BLOCKS] = out[:HALF_DELAYS, cols]
                corr[at : at + HALF_DELAYS, BLOCKS:] = out[HALF_DELAYS:, cols]
        x = dot(corr[...], dop_ref[k])
        x_re, x_im = x[:, :DOPPLER], x[:, DOPPLER:]
        power = (x_re * x_re + x_im * x_im) * (1.0 / (4 * BLOCKS))
        power = functools.reduce(
            jnp.add, [power[n * rows : (n + 1) * rows] for n in range(len(segments))]
        )
        emit(k, power.reshape(count, HALF_DELAYS, DOPPLER))


def emit_halves(chunks, own_ref, send_ref):
    each = DELAYS // chunks

    def emit(k, power):
        own_ref[k] = power[:, :each]
        for n in range(1, chunks // 2):
            send_ref[n - 1, k] = power[:, n * each : (n + 1) * each].astype(jnp.bfloat16)

    return emit


def first_kernel(
    params, rtab, mine, other, stab, s_ref, lags, dops, r_ref, part_ref, padded, spec, prods, corrs
):
    write_ref_spectra(params, rtab, mine, other, r_ref, padded)

    def emit(k, power):
        part_ref[k] = power

    sum_powers(stab, [(s_ref, r_ref)], lags, dops, spec, prods, corrs, emit)


def second_kernel(
    chunks, params, rtab, mine, other, stab, s_ref, lags, dops, part_ref, r_ref, own_ref, send_ref, padded, spec, prods, corrs
):
    write_ref_spectra(params, rtab, mine, other, r_ref, padded)
    store = emit_halves(chunks, own_ref, send_ref)
    emit = lambda k, power: store(k, power + part_ref[k])
    sum_powers(stab, [(s_ref, r_ref)], lags, dops, spec, prods, corrs, emit)


def both_kernel(
    chunks, stab, here, there, r_here, r_there, lags, dops, own_ref, send_ref, spec, prods, corrs
):
    emit = emit_halves(chunks, own_ref, send_ref)
    sum_powers(stab, [(here, r_here), (there, r_there)], lags, dops, spec, prods, corrs, emit)


def call_powers(kernel, name, args, out_shape, count, segments, spectra):
    padded = [pltpu.VMEM((BLOCKS + 2 * PAD, PAIR), jnp.float32)]
    return pl.pallas_call(
        kernel,
        in_specs=[SMEM if a.ndim == 1 else VMEM for a in args],
        out_specs=[VMEM] * len(out_shape),
        out_shape=out_shape,
        scratch_shapes=(padded if spectra else [])
        + [
            pltpu.VMEM((segments, 2 * FFT, count * BLOCKS), jnp.float32),
            pltpu.VMEM((segments, 2 * FFT, count * BLOCKS), jnp.bfloat16),
            pltpu.VMEM((2, segments * count * HALF_DELAYS, 2 * BLOCKS), jnp.bfloat16),
        ],
        compiler_params=pltpu.CompilerParams(vmem_limit_bytes=VMEM_LIMIT),
        cost_estimate=pl.CostEstimate(
            flops=segments * count * TX * 4 * 768 * 65536, bytes_accessed=6 << 20, transcendentals=0
        ),
        name=name,
    )(*args)


def swap(value, axis, flip):
    size = lax.axis_size(axis)
    return lax.ppermute(value, axis, [(i, i ^ flip) for i in range(size)])


def shards(voltages, surv_taps, ref_taps, tx_owner, delay_start, doppler_start):
    beams_here = voltages.shape[1]
    n_beam = lax.axis_size("beam")
    n_seg = lax.axis_size("seg")
    segments_all = n_seg * voltages.shape[2]
    ids = jnp.stack([lax.axis_index("beam"), lax.axis_index("seg")]).astype(jnp.int32)
    volts = voltages.reshape(2, beams_here, voltages.shape[3])
    out = decimate(
        volts,
        surv_taps.reshape(1, TAPS),
        ref_taps.reshape(1, TAPS),
        ids,
        tx_owner,
        delay_start,
        doppler_start,
    )
    surv, (keep, send, params) = out[:GROUPS], out[GROUPS:]
    half = keep + swap(send, "beam", 1)
    half, surv, params = lax.optimization_barrier((half, surv, params))
    got = [swap(half, "beam", flip) for flip in range(2, n_beam, 2)]
    there = [swap(s, "seg", 1) for s in surv]
    lags, dops = make_tables(params, n_seg)
    got, lags, dops = lax.optimization_barrier((got, lags, dops))
    half = functools.reduce(jnp.add, got, half)
    other = swap(half, "beam", 1)
    leaving, there[0] = lax.optimization_barrier((half, there[0]))
    far = swap(leaving, "seg", 1)
    far_other = swap(other, "seg", 1)
    stab, rtab = jnp.asarray(surv_fourier()), jnp.asarray(ref_fourier())
    count = beams_here // GROUPS
    each = DELAYS // n_seg
    r_shape = jax.ShapeDtypeStruct((TX, 2 * FFT, BLOCKS), jnp.float32)
    part_shape = jax.ShapeDtypeStruct((TX, count, HALF_DELAYS, DOPPLER), jnp.float32)
    halves = [
        jax.ShapeDtypeStruct((TX, count, each, DOPPLER), jnp.float32),
        jax.ShapeDtypeStruct((n_seg // 2 - 1, TX, count, each, DOPPLER), jnp.bfloat16),
    ]
    r_here, part = call_powers(
        first_kernel,
        "first",
        (params, rtab, half, other, stab, surv[0], lags, dops),
        [r_shape, part_shape],
        count,
        1,
        True,
    )
    far, far_other, there[1] = lax.optimization_barrier((far, far_other, there[1]))
    r_there, *sums = call_powers(
        functools.partial(second_kernel, n_seg),
        "second",
        (params, rtab, far, far_other, stab, there[0], lags, dops, part),
        [r_shape] + halves,
        count,
        1,
        True,
    )
    maps = []
    for g in range(GROUPS):
        if g > 0:
            sums = call_powers(
                functools.partial(both_kernel, n_seg),
                "both",
                (stab, surv[g], there[g], r_here, r_there, lags, dops),
                halves,
                count,
                2,
                False,
            )
        total, outgoing = sums
        for n in range(1, n_seg // 2):
            total = total + swap(outgoing[n - 1], "seg", 2 * n).astype(jnp.float32)
        maps.append(total / segments_all)
    return jnp.concatenate(maps, axis=1)


def solution(mesh):
    return jax.shard_map(
        shards,
        mesh=mesh,
        in_specs=(P(None, "beam", "seg", None), P(), P(), P(), P(), P()),
        out_specs=P(None, "beam", "seg", None),
        check_vma=False,
    )
```

```python
import functools

import jax
import jax.numpy as jnp
import ml_dtypes
import numpy as np
from jax import lax
from jax.experimental import pallas as pl
from jax.experimental.pallas import tpu as pltpu
from jax.sharding import PartitionSpec as P

TX = 4
HALF_TX = TX // 2
DECIM = 4
TAPS = 32
BLOCK_LEN = 64
BLOCKS = 256
DELAYS = 128
DOPPLER = 128
FFT = 256
STRIDE = DECIM * BLOCK_LEN
LEAD = 128
REACH = LEAD + STRIDE
PAIR = 2 * BLOCK_LEN
GROUPS = 4
LANES = 128
LANE_BLOCKS = 2 * FFT // LANES
HALF_DELAYS = DELAYS // 2
VMEM_LIMIT = 24 * 1024 * 1024

SMEM = pl.BlockSpec(memory_space=pltpu.SMEM)
VMEM = pl.BlockSpec(memory_space=pltpu.VMEM)
HBM = pl.BlockSpec(memory_space=pltpu.HBM)


def split_bf16(table):
    hi = table.astype(ml_dtypes.bfloat16)
    lo = (table - hi.astype(np.float64)).astype(ml_dtypes.bfloat16)
    return hi, lo


def fourier(samples):
    angle = 2 * np.pi / FFT * (np.outer(np.arange(FFT), samples) % FFT)
    cos, sin = np.cos(angle), np.sin(angle)
    return np.block([[cos, sin], [-sin, cos]])


def surv_fourier():
    hi, lo = split_bf16(fourier(np.arange(BLOCK_LEN)))
    return np.concatenate([hi, lo], axis=1)


def ref_fourier():
    parts = [fourier(np.arange(BLOCK_LEN) + BLOCK_LEN * e) for e in range(4)]
    hi, lo = split_bf16(np.concatenate(parts, axis=1))
    return np.concatenate([hi, lo], axis=1)


def in_lane_blocks(both):
    parts, rows, _ = both.shape
    return both.astype(np.float32).reshape(parts, rows, LANE_BLOCKS, LANES).swapaxes(1, 2)


def lag_table():
    lags = 191 - np.arange(192)
    angle = 2 * np.pi / FFT * (np.outer(lags, np.arange(FFT)) % FFT)
    cos, sin = np.cos(angle), np.sin(angle)
    scale = 1.0 / (FFT * np.sqrt(BLOCK_LEN))
    both = np.stack([np.concatenate([cos, sin], 1), np.concatenate([-sin, cos], 1)])
    both = both.astype(ml_dtypes.bfloat16).astype(np.float64) * scale
    return in_lane_blocks(both)


def doppler_table():
    freqs = np.arange(BLOCKS) - BLOCKS // 2
    angle = 2 * np.pi / BLOCKS * (np.outer(freqs, np.arange(BLOCKS)) % BLOCKS)
    cos, sin = np.cos(angle), np.sin(angle)
    both = np.stack([np.concatenate([cos, sin], 1), np.concatenate([-sin, cos], 1)])
    return in_lane_blocks(both.astype(ml_dtypes.bfloat16))


def nt_dot(left, right):
    return lax.dot_general(
        left, right, (((1,), (1,)), ((), ())), preferred_element_type=jnp.float32
    )


def dot(left, right):
    return jnp.dot(left, right, preferred_element_type=jnp.float32)


def decimate_kernel(beams, ids, owner, delay, doppler, staps, rtaps, volts, *refs):
    s_refs, refs = refs[:GROUPS], refs[GROUPS:]
    keep_ref, send_ref, params, x, taps, small, band, all_s, all_r, sems, small_sems = refs
    chunks = sems.shape[0]
    raw = volts.shape[2]
    wide = raw // chunks
    rows = wide // STRIDE
    blocks = raw // STRIDE
    smalls = [
        pltpu.make_async_copy(ref, small.at[n], small_sems.at[n])
        for n, ref in enumerate((owner, delay, doppler))
    ]
    smalls += [
        pltpu.make_async_copy(ref, taps.at[n], small_sems.at[3 + n])
        for n, ref in enumerate((staps, rtaps))
    ]
    copies = [
        pltpu.make_async_copy(
            volts.at[:, :, pl.ds(n * wide, wide)],
            x.at[:, :, pl.ds(LEAD + n * wide, wide)],
            sems.at[n],
        )
        for n in range(chunks)
    ]
    for copy in smalls + copies:
        copy.start()
    x[:, :, :LEAD] = jnp.zeros((2, beams, LEAD), jnp.bfloat16)
    for copy in smalls:
        copy.wait()

    shape = (REACH, PAIR)
    q = lax.broadcasted_iota(jnp.int32, shape, 0)
    lane = lax.broadcasted_iota(jnp.int32, shape, 1)
    tap = LEAD + DECIM * (lane % BLOCK_LEN) - q
    first = lane < BLOCK_LEN
    one, two = taps[0].astype(jnp.float32), taps[1].astype(jnp.float32)
    both = jnp.zeros(shape, jnp.float32)
    for t in range(TAPS):
        row = jnp.where(first[:1], one[:, t : t + 1], two[:, t : t + 1])
        both = jnp.where(tap == t, row, both)
    turned = pltpu.roll(both, BLOCK_LEN, 1)
    zero = jnp.zeros(shape, jnp.float32)
    band[:REACH, :PAIR] = jnp.where(first, both, zero).astype(jnp.bfloat16)
    band[REACH:, :PAIR] = jnp.where(first, zero, turned).astype(jnp.bfloat16)
    band[:REACH, PAIR:] = jnp.where(first, turned, zero).astype(jnp.bfloat16)
    band[REACH:, PAIR:] = jnp.where(first, zero, both).astype(jnp.bfloat16)
    for k in range(TX):
        params[k] = small[1, k]
        params[TX + k] = small[2, k]
    params[2 * TX] = ids[0]
    params[2 * TX + 1] = ids[1]

    def step(n, _):
        pltpu.make_async_copy(
            volts.at[:, :, pl.ds(n * wide, wide)],
            x.at[:, :, pl.ds(LEAD + n * wide, wide)],
            sems.at[n],
        ).wait()
        parts = []
        for c in range(2):
            starts = [pl.multiple_of(n * wide + l * STRIDE, STRIDE) for l in range(rows)]
            parts.append(jnp.concatenate([x[c, :, pl.ds(at, REACH)] for at in starts], axis=0))
        out = dot(jnp.concatenate(parts, axis=1), band[...])
        span = pl.ds(pl.multiple_of(n * rows * beams, rows * beams), rows * beams)
        all_s[span] = out[:, :PAIR]
        all_r[span] = out[:, PAIR:]
        count = beams // GROUPS
        here = pl.ds(pl.multiple_of(n * rows, rows), rows)
        for b in range(beams):
            picked = all_s[pl.ds(n * rows * beams + b, rows, stride=beams), :]
            s_refs[b // count][b % count, here] = picked.astype(jnp.bfloat16)
        return 0

    lax.fori_loop(0, chunks, step, 0)
    core = ids[0] % 2
    for ref, first_tx in ((keep_ref, core * HALF_TX), (send_ref, (1 - core) * HALF_TX)):
        for k in range(HALF_TX):
            beam = small[0, first_tx + k]
            picked = all_r[pl.ds(beam % beams, blocks, stride=beams), :]
            ref[k] = jnp.where(beam // beams == ids[0], picked, 0.0).astype(jnp.bfloat16)


def decimate(volts, staps, rtaps, ids, owner, delay, doppler):
    beams, raw = volts.shape[1:]
    blocks = raw // STRIDE
    count = beams // GROUPS
    chunks = 1
    arrays = (owner, delay, doppler, staps, rtaps, volts)
    shape = lambda n: jax.ShapeDtypeStruct((n, blocks, PAIR), jnp.bfloat16)
    return pl.pallas_call(
        functools.partial(decimate_kernel, beams),
        in_specs=[SMEM] + [HBM] * 6,
        out_specs=[VMEM] * (GROUPS + 2) + [SMEM],
        out_shape=[shape(count)] * GROUPS
        + [shape(HALF_TX)] * 2
        + [jax.ShapeDtypeStruct((2 * TX + 2,), jnp.int32)],
        scratch_shapes=[
            pltpu.VMEM((2, beams, LEAD + raw), jnp.bfloat16),
            pltpu.VMEM((2, 1, TAPS), jnp.bfloat16),
            pltpu.SMEM((3, TX), jnp.int32),
            pltpu.VMEM((2 * REACH, 2 * PAIR), jnp.bfloat16),
            pltpu.VMEM((blocks * beams, PAIR), jnp.float32),
            pltpu.VMEM((blocks * beams, PAIR), jnp.float32),
            pltpu.SemaphoreType.DMA((chunks,)),
            pltpu.SemaphoreType.DMA((5,)),
        ],
        compiler_params=pltpu.CompilerParams(vmem_limit_bytes=VMEM_LIMIT),
        name="decimate",
    )(ids, *(pltpu.with_memory_space_constraint(a, pltpu.HBM) for a in arrays))


def tables_kernel(chunks, params, lag_ref, dop_ref, lags, dops):
    each = DELAYS // chunks
    for k in range(TX):
        base = (params[k] + DELAYS - 1) % BLOCK_LEN
        for part in range(2):
            for n in range(chunks // 2):
                chunk = params[2 * TX + 1] ^ (2 * n)
                at = part * HALF_DELAYS + n * each
                for q in range(LANE_BLOCKS):
                    picked = lag_ref[part, q, pl.ds(base + chunk * each, each), :]
                    lags[k, at : at + each, q * LANES : (q + 1) * LANES] = picked.astype(jnp.bfloat16)
            for q in range(LANE_BLOCKS):
                picked = dop_ref[part, q, pl.ds(params[TX + k], DOPPLER), :].T.astype(jnp.bfloat16)
                dops[k, q * LANES : (q + 1) * LANES, part * DOPPLER : (part + 1) * DOPPLER] = picked


def make_tables(params, chunks):
    return pl.pallas_call(
        functools.partial(tables_kernel, chunks),
        in_specs=[SMEM, VMEM, VMEM],
        out_specs=[VMEM, VMEM],
        out_shape=[
            jax.ShapeDtypeStruct((TX, DELAYS, 2 * FFT), jnp.bfloat16),
            jax.ShapeDtypeStruct((TX, 2 * BLOCKS, 2 * DOPPLER), jnp.bfloat16),
        ],
        compiler_params=pltpu.CompilerParams(vmem_limit_bytes=VMEM_LIMIT),
        name="tables",
    )(params, jnp.asarray(lag_table()), jnp.asarray(doppler_table()))


PAD = 8


def write_ref_spectra(params, table_ref, mine_ref, other_ref, out_ref, padded):
    core = params[2 * TX] % 2
    padded[:PAD] = jnp.zeros((PAD, PAIR), jnp.float32)
    padded[PAD + BLOCKS :] = jnp.zeros((PAD, PAIR), jnp.float32)
    for k in range(TX):
        here = core == k // HALF_TX
        ref = jnp.where(here, mine_ref[k % HALF_TX], other_ref[k % HALF_TX])
        padded[PAD : PAD + BLOCKS] = ref.astype(jnp.float32)
        start = PAD - 1 - (params[k] + DELAYS - 1) // BLOCK_LEN
        window = jnp.concatenate(
            [padded[pl.ds(start + e, BLOCKS), :].astype(jnp.bfloat16) for e in range(4)], axis=1
        )
        out_ref[k] = nt_dot(table_ref[...], jnp.concatenate([window, window], axis=1))


def sum_powers(table_ref, segments, lag_ref, dop_ref, spec, prods, corrs, emit):
    count = segments[0][0].shape[0]
    rows = count * HALF_DELAYS
    for n, (s_ref, _) in enumerate(segments):
        s = s_ref[...].reshape(count * BLOCKS, PAIR)
        spec[n] = nt_dot(table_ref[...], jnp.concatenate([s, s], axis=1))
    for k in range(TX):
        corr = corrs.at[k % 2]
        for n, (_, r_ref) in enumerate(segments):
            r_re, r_im = r_ref[k, :FFT], r_ref[k, FFT:]
            prod = prods.at[n]
            for b in range(count):
                cols = slice(b * BLOCKS, (b + 1) * BLOCKS)
                s_re, s_im = spec[n, :FFT, cols], spec[n, FFT:, cols]
                prod[:FFT, cols] = (s_re * r_re + s_im * r_im).astype(jnp.bfloat16)
                prod[FFT:, cols] = (s_im * r_re - s_re * r_im).astype(jnp.bfloat16)
            out = dot(lag_ref[k], prod[...]).astype(jnp.bfloat16)
            for b in range(count):
                cols = slice(b * BLOCKS, (b + 1) * BLOCKS)
                at = n * rows + b * HALF_DELAYS
                corr[at : at + HALF_DELAYS, :BLOCKS] = out[:HALF_DELAYS, cols]
                corr[at : at + HALF_DELAYS, BLOCKS:] = out[HALF_DELAYS:, cols]
        x = dot(corr[...], dop_ref[k])
        x_re, x_im = x[:, :DOPPLER], x[:, DOPPLER:]
        power = (x_re * x_re + x_im * x_im) * (1.0 / (4 * BLOCKS))
        power = functools.reduce(
            jnp.add, [power[n * rows : (n + 1) * rows] for n in range(len(segments))]
        )
        emit(k, power.reshape(count, HALF_DELAYS, DOPPLER))


def emit_halves(chunks, own_ref, send_ref):
    each = DELAYS // chunks

    def emit(k, power):
        own_ref[k] = power[:, :each]
        for n in range(1, chunks // 2):
            send_ref[n - 1, k] = power[:, n * each : (n + 1) * each].astype(jnp.bfloat16)

    return emit


def first_kernel(
    params, rtab, mine, other, stab, s_ref, lags, dops, r_ref, part_ref, padded, spec, prods, corrs
):
    write_ref_spectra(params, rtab, mine, other, r_ref, padded)

    def emit(k, power):
        part_ref[k] = power

    sum_powers(stab, [(s_ref, r_ref)], lags, dops, spec, prods, corrs, emit)


def second_kernel(
    chunks, params, rtab, mine, other, stab, s_ref, lags, dops, part_ref, r_ref, own_ref, send_ref, padded, spec, prods, corrs
):
    write_ref_spectra(params, rtab, mine, other, r_ref, padded)
    store = emit_halves(chunks, own_ref, send_ref)
    emit = lambda k, power: store(k, power + part_ref[k])
    sum_powers(stab, [(s_ref, r_ref)], lags, dops, spec, prods, corrs, emit)


def both_kernel(
    chunks, stab, here, there, r_here, r_there, lags, dops, own_ref, send_ref, spec, prods, corrs
):
    emit = emit_halves(chunks, own_ref, send_ref)
    sum_powers(stab, [(here, r_here), (there, r_there)], lags, dops, spec, prods, corrs, emit)


def call_powers(kernel, name, args, out_shape, count, segments, spectra):
    padded = [pltpu.VMEM((BLOCKS + 2 * PAD, PAIR), jnp.float32)]
    return pl.pallas_call(
        kernel,
        in_specs=[SMEM if a.ndim == 1 else VMEM for a in args],
        out_specs=[VMEM] * len(out_shape),
        out_shape=out_shape,
        scratch_shapes=(padded if spectra else [])
        + [
            pltpu.VMEM((segments, 2 * FFT, count * BLOCKS), jnp.float32),
            pltpu.VMEM((segments, 2 * FFT, count * BLOCKS), jnp.bfloat16),
            pltpu.VMEM((2, segments * count * HALF_DELAYS, 2 * BLOCKS), jnp.bfloat16),
        ],
        compiler_params=pltpu.CompilerParams(vmem_limit_bytes=VMEM_LIMIT),
        cost_estimate=pl.CostEstimate(
            flops=segments * count * TX * 4 * 768 * 65536, bytes_accessed=6 << 20, transcendentals=0
        ),
        name=name,
    )(*args)


def swap(value, axis, flip):
    size = lax.axis_size(axis)
    return lax.ppermute(value, axis, [(i, i ^ flip) for i in range(size)])


def shards(voltages, surv_taps, ref_taps, tx_owner, delay_start, doppler_start):
    beams_here = voltages.shape[1]
    n_beam = lax.axis_size("beam")
    n_seg = lax.axis_size("seg")
    segments_all = n_seg * voltages.shape[2]
    ids = jnp.stack([lax.axis_index("beam"), lax.axis_index("seg")]).astype(jnp.int32)
    volts = voltages.reshape(2, beams_here, voltages.shape[3])
    out = decimate(
        volts,
        surv_taps.reshape(1, TAPS),
        ref_taps.reshape(1, TAPS),
        ids,
        tx_owner,
        delay_start,
        doppler_start,
    )
    surv, (keep, send, params) = out[:GROUPS], out[GROUPS:]
    half = keep + swap(send, "beam", 1)
    half, surv, params = lax.optimization_barrier((half, surv, params))
    got = [swap(half, "beam", flip) for flip in range(2, n_beam, 2)]
    there = [swap(surv[0], "seg", 1)]
    lags, dops = make_tables(params, n_seg)
    got, lags, dops = lax.optimization_barrier((got, lags, dops))
    half = functools.reduce(jnp.add, got, half)
    other = swap(half, "beam", 1)
    leaving, there[0] = lax.optimization_barrier((half, there[0]))
    far = swap(leaving, "seg", 1)
    far_other = swap(other, "seg", 1)
    stab, rtab = jnp.asarray(surv_fourier()), jnp.asarray(ref_fourier())
    count = beams_here // GROUPS
    each = DELAYS // n_seg
    r_shape = jax.ShapeDtypeStruct((TX, 2 * FFT, BLOCKS), jnp.float32)
    part_shape = jax.ShapeDtypeStruct((TX, count, HALF_DELAYS, DOPPLER), jnp.float32)
    halves = [
        jax.ShapeDtypeStruct((TX, count, each, DOPPLER), jnp.float32),
        jax.ShapeDtypeStruct((n_seg // 2 - 1, TX, count, each, DOPPLER), jnp.bfloat16),
    ]
    r_here, part = call_powers(
        first_kernel,
        "first",
        (params, rtab, half, other, stab, surv[0], lags, dops),
        [r_shape, part_shape],
        count,
        1,
        True,
    )
    surv, part = lax.optimization_barrier((surv, part))
    there += [swap(s, "seg", 1) for s in surv[1:]]
    r_there, *sums = call_powers(
        functools.partial(second_kernel, n_seg),
        "second",
        (params, rtab, far, far_other, stab, there[0], lags, dops, part),
        [r_shape] + halves,
        count,
        1,
        True,
    )
    maps = []
    for g in range(GROUPS):
        if g > 0:
            sums = call_powers(
                functools.partial(both_kernel, n_seg),
                "both",
                (stab, surv[g], there[g], r_here, r_there, lags, dops),
                halves,
                count,
                2,
                False,
            )
        total, outgoing = sums
        for n in range(1, n_seg // 2):
            total = total + swap(outgoing[n - 1], "seg", 2 * n).astype(jnp.float32)
        maps.append(total / segments_all)
    return jnp.concatenate(maps, axis=1)


def solution(mesh):
    return jax.shard_map(
        shards,
        mesh=mesh,
        in_specs=(P(None, "beam", "seg", None), P(), P(), P(), P(), P()),
        out_specs=P(None, "beam", "seg", None),
        check_vma=False,
    )
```

```python
import functools

import jax
import jax.numpy as jnp
import ml_dtypes
import numpy as np
from jax import lax
from jax.experimental import pallas as pl
from jax.experimental.pallas import tpu as pltpu
from jax.sharding import PartitionSpec as P

TX = 4
HALF_TX = TX // 2
DECIM = 4
TAPS = 32
BLOCK_LEN = 64
BLOCKS = 256
DELAYS = 128
DOPPLER = 128
FFT = 256
STRIDE = DECIM * BLOCK_LEN
LEAD = 128
REACH = LEAD + STRIDE
PAIR = 2 * BLOCK_LEN
GROUPS = (4, 4)
LANES = 128
LANE_BLOCKS = 2 * FFT // LANES
VMEM_LIMIT = 24 * 1024 * 1024

SMEM = pl.BlockSpec(memory_space=pltpu.SMEM)
VMEM = pl.BlockSpec(memory_space=pltpu.VMEM)
HBM = pl.BlockSpec(memory_space=pltpu.HBM)


def split_bf16(table):
    hi = table.astype(ml_dtypes.bfloat16)
    lo = (table - hi.astype(np.float64)).astype(ml_dtypes.bfloat16)
    return hi, lo


def fourier(samples):
    angle = 2 * np.pi / FFT * (np.outer(np.arange(FFT), samples) % FFT)
    cos, sin = np.cos(angle), np.sin(angle)
    return np.block([[cos, sin], [-sin, cos]])


def surv_fourier():
    hi, lo = split_bf16(fourier(np.arange(BLOCK_LEN)))
    return np.concatenate([hi, lo], axis=1)


def ref_fourier():
    parts = [fourier(np.arange(BLOCK_LEN) + BLOCK_LEN * e) for e in range(4)]
    hi, lo = split_bf16(np.concatenate(parts, axis=1))
    return np.concatenate([hi, lo], axis=1)


def in_lane_blocks(both):
    parts, rows, _ = both.shape
    return both.astype(np.float32).reshape(parts, rows, LANE_BLOCKS, LANES).swapaxes(1, 2)


def lag_table():
    lags = 191 - np.arange(192)
    angle = 2 * np.pi / FFT * (np.outer(lags, np.arange(FFT)) % FFT)
    cos, sin = np.cos(angle), np.sin(angle)
    scale = 1.0 / (FFT * np.sqrt(BLOCK_LEN))
    both = np.stack([np.concatenate([cos, sin], 1), np.concatenate([-sin, cos], 1)])
    both = both.astype(ml_dtypes.bfloat16).astype(np.float64) * scale
    return in_lane_blocks(both)


def doppler_table():
    freqs = np.arange(BLOCKS) - BLOCKS // 2
    angle = 2 * np.pi / BLOCKS * (np.outer(freqs, np.arange(BLOCKS)) % BLOCKS)
    cos, sin = np.cos(angle), np.sin(angle)
    both = np.stack([np.concatenate([cos, sin], 1), np.concatenate([-sin, cos], 1)])
    return in_lane_blocks(both.astype(ml_dtypes.bfloat16))


def nt_dot(left, right):
    return lax.dot_general(
        left, right, (((1,), (1,)), ((), ())), preferred_element_type=jnp.float32
    )


def dot(left, right):
    return jnp.dot(left, right, preferred_element_type=jnp.float32)


def decimate_kernel(beams, ids, owner, delay, doppler, staps, rtaps, volts, *refs):
    here_ref, give_ref, keep_ref, send_ref, params, x, taps, small, band, all_s, all_r, sems, small_sems = refs
    chunks = sems.shape[0]
    raw = volts.shape[2]
    wide = raw // chunks
    rows = wide // STRIDE
    blocks = raw // STRIDE
    smalls = [
        pltpu.make_async_copy(ref, small.at[n], small_sems.at[n])
        for n, ref in enumerate((owner, delay, doppler))
    ]
    smalls += [
        pltpu.make_async_copy(ref, taps.at[n], small_sems.at[3 + n])
        for n, ref in enumerate((staps, rtaps))
    ]
    copies = [
        pltpu.make_async_copy(
            volts.at[:, :, pl.ds(n * wide, wide)],
            x.at[:, :, pl.ds(LEAD + n * wide, wide)],
            sems.at[n],
        )
        for n in range(chunks)
    ]
    for copy in smalls + copies:
        copy.start()
    x[:, :, :LEAD] = jnp.zeros((2, beams, LEAD), jnp.bfloat16)
    for copy in smalls:
        copy.wait()

    shape = (REACH, PAIR)
    q = lax.broadcasted_iota(jnp.int32, shape, 0)
    lane = lax.broadcasted_iota(jnp.int32, shape, 1)
    tap = LEAD + DECIM * (lane % BLOCK_LEN) - q
    first = lane < BLOCK_LEN
    one, two = taps[0].astype(jnp.float32), taps[1].astype(jnp.float32)
    both = jnp.zeros(shape, jnp.float32)
    for t in range(TAPS):
        row = jnp.where(first[:1], one[:, t : t + 1], two[:, t : t + 1])
        both = jnp.where(tap == t, row, both)
    turned = pltpu.roll(both, BLOCK_LEN, 1)
    zero = jnp.zeros(shape, jnp.float32)
    band[:REACH, :PAIR] = jnp.where(first, both, zero).astype(jnp.bfloat16)
    band[REACH:, :PAIR] = jnp.where(first, zero, turned).astype(jnp.bfloat16)
    band[:REACH, PAIR:] = jnp.where(first, turned, zero).astype(jnp.bfloat16)
    band[REACH:, PAIR:] = jnp.where(first, zero, both).astype(jnp.bfloat16)
    for k in range(TX):
        params[k] = small[1, k]
        params[TX + k] = small[2, k]
    params[2 * TX] = ids[0]
    params[2 * TX + 1] = ids[1]

    def step(n, _):
        pltpu.make_async_copy(
            volts.at[:, :, pl.ds(n * wide, wide)],
            x.at[:, :, pl.ds(LEAD + n * wide, wide)],
            sems.at[n],
        ).wait()
        parts = []
        for c in range(2):
            starts = [pl.multiple_of(n * wide + l * STRIDE, STRIDE) for l in range(rows)]
            parts.append(jnp.concatenate([x[c, :, pl.ds(at, REACH)] for at in starts], axis=0))
        out = dot(jnp.concatenate(parts, axis=1), band[...])
        span = pl.ds(pl.multiple_of(n * rows * beams, rows * beams), rows * beams)
        all_s[span] = out[:, :PAIR]
        all_r[span] = out[:, PAIR:]
        here = pl.ds(pl.multiple_of(n * rows, rows), rows)
        part = ids[1] % 2
        half = beams // 2
        for s_ref, at in ((here_ref, part * half), (give_ref, (1 - part) * half)):
            for b in range(half):
                picked = all_s[pl.ds(n * rows * beams + at + b, rows, stride=beams), :]
                s_ref[b, here] = picked.astype(jnp.bfloat16)
        return 0

    lax.fori_loop(0, chunks, step, 0)
    core = ids[0] % 2
    for ref, first_tx in ((keep_ref, core * HALF_TX), (send_ref, (1 - core) * HALF_TX)):
        for k in range(HALF_TX):
            beam = small[0, first_tx + k]
            picked = all_r[pl.ds(beam % beams, blocks, stride=beams), :]
            ref[k] = jnp.where(beam // beams == ids[0], picked, 0.0).astype(jnp.bfloat16)


def decimate(volts, staps, rtaps, ids, owner, delay, doppler):
    beams, raw = volts.shape[1:]
    blocks = raw // STRIDE
    chunks = 1
    arrays = (owner, delay, doppler, staps, rtaps, volts)
    shape = lambda n: jax.ShapeDtypeStruct((n, blocks, PAIR), jnp.bfloat16)
    return pl.pallas_call(
        functools.partial(decimate_kernel, beams),
        in_specs=[SMEM] + [HBM] * 6,
        out_specs=[VMEM] * 4 + [SMEM],
        out_shape=[shape(beams // 2)] * 2
        + [shape(HALF_TX)] * 2
        + [jax.ShapeDtypeStruct((2 * TX + 2,), jnp.int32)],
        scratch_shapes=[
            pltpu.VMEM((2, beams, LEAD + raw), jnp.bfloat16),
            pltpu.VMEM((2, 1, TAPS), jnp.bfloat16),
            pltpu.SMEM((3, TX), jnp.int32),
            pltpu.VMEM((2 * REACH, 2 * PAIR), jnp.bfloat16),
            pltpu.VMEM((blocks * beams, PAIR), jnp.float32),
            pltpu.VMEM((blocks * beams, PAIR), jnp.float32),
            pltpu.SemaphoreType.DMA((chunks,)),
            pltpu.SemaphoreType.DMA((5,)),
        ],
        compiler_params=pltpu.CompilerParams(vmem_limit_bytes=VMEM_LIMIT),
        name="decimate",
    )(ids, *(pltpu.with_memory_space_constraint(a, pltpu.HBM) for a in arrays))


def tables_kernel(chunks, params, lag_ref, dop_ref, lags, dops):
    each = DELAYS // chunks
    for k in range(TX):
        base = (params[k] + DELAYS - 1) % BLOCK_LEN
        for part in range(2):
            for n in range(chunks):
                chunk = params[2 * TX + 1] ^ n
                at = part * DELAYS + n * each
                for q in range(LANE_BLOCKS):
                    picked = lag_ref[part, q, pl.ds(base + chunk * each, each), :]
                    lags[k, at : at + each, q * LANES : (q + 1) * LANES] = picked.astype(jnp.bfloat16)
            for q in range(LANE_BLOCKS):
                picked = dop_ref[part, q, pl.ds(params[TX + k], DOPPLER), :].T.astype(jnp.bfloat16)
                dops[k, q * LANES : (q + 1) * LANES, part * DOPPLER : (part + 1) * DOPPLER] = picked


def make_tables(params, chunks):
    return pl.pallas_call(
        functools.partial(tables_kernel, chunks),
        in_specs=[SMEM, VMEM, VMEM],
        out_specs=[VMEM, VMEM],
        out_shape=[
            jax.ShapeDtypeStruct((TX, 2 * DELAYS, 2 * FFT), jnp.bfloat16),
            jax.ShapeDtypeStruct((TX, 2 * BLOCKS, 2 * DOPPLER), jnp.bfloat16),
        ],
        compiler_params=pltpu.CompilerParams(vmem_limit_bytes=VMEM_LIMIT),
        name="tables",
    )(params, jnp.asarray(lag_table()), jnp.asarray(doppler_table()))


PAD = 8


def write_ref_spectra(params, table_ref, mine_ref, other_ref, out_ref, padded):
    core = params[2 * TX] % 2
    padded[:PAD] = jnp.zeros((PAD, PAIR), jnp.float32)
    padded[PAD + BLOCKS :] = jnp.zeros((PAD, PAIR), jnp.float32)
    for k in range(TX):
        here = core == k // HALF_TX
        ref = jnp.where(here, mine_ref[k % HALF_TX], other_ref[k % HALF_TX])
        padded[PAD : PAD + BLOCKS] = ref.astype(jnp.float32)
        start = PAD - 1 - (params[k] + DELAYS - 1) // BLOCK_LEN
        window = jnp.concatenate(
            [padded[pl.ds(start + e, BLOCKS), :].astype(jnp.bfloat16) for e in range(4)], axis=1
        )
        out_ref[k] = nt_dot(table_ref[...], jnp.concatenate([window, window], axis=1))


def surv_spectrum(table_ref, s):
    return nt_dot(table_ref[...], jnp.concatenate([s, s], axis=1))


def surv_spectra_kernel(table_ref, s_ref, out_ref):
    for b in range(s_ref.shape[0]):
        out_ref[b] = surv_spectrum(table_ref, s_ref[b])


def surv_spectra(table, surv, name):
    return pl.pallas_call(
        surv_spectra_kernel,
        in_specs=[VMEM] * 2,
        out_specs=VMEM,
        out_shape=jax.ShapeDtypeStruct((surv.shape[0], 2 * FFT, BLOCKS), jnp.float32),
        compiler_params=pltpu.CompilerParams(vmem_limit_bytes=VMEM_LIMIT),
        name=name,
    )(table, surv)


def sum_powers(segments, lag_ref, dop_ref, prods, corrs, emit):
    count = len(segments[0][0])
    rows = count * DELAYS
    for k in range(TX):
        corr = corrs.at[k % 2]
        for n, (beams, r_ref) in enumerate(segments):
            r_re, r_im = r_ref[k, :FFT], r_ref[k, FFT:]
            prod = prods.at[n]
            for b, (s_ref, at) in enumerate(beams):
                cols = slice(b * BLOCKS, (b + 1) * BLOCKS)
                s_re, s_im = s_ref[at, :FFT], s_ref[at, FFT:]
                prod[:FFT, cols] = (s_re * r_re + s_im * r_im).astype(jnp.bfloat16)
                prod[FFT:, cols] = (s_im * r_re - s_re * r_im).astype(jnp.bfloat16)
            out = dot(lag_ref[k], prod[...]).astype(jnp.bfloat16)
            for b in range(count):
                cols = slice(b * BLOCKS, (b + 1) * BLOCKS)
                at = n * rows + b * DELAYS
                corr[at : at + DELAYS, :BLOCKS] = out[:DELAYS, cols]
                corr[at : at + DELAYS, BLOCKS:] = out[DELAYS:, cols]
        x = dot(corr[...], dop_ref[k])
        x_re, x_im = x[:, :DOPPLER], x[:, DOPPLER:]
        power = (x_re * x_re + x_im * x_im) * (1.0 / (4 * BLOCKS))
        power = functools.reduce(
            jnp.add, [power[n * rows : (n + 1) * rows] for n in range(len(segments))]
        )
        emit(k, power.reshape(count, DELAYS, DOPPLER))


def emit_chunks(own_ref, send_refs):
    each = own_ref.shape[2]

    def emit(k, power):
        own_ref[k] = power[:, :each]
        for n, ref in enumerate(send_refs):
            ref[k] = power[:, (n + 1) * each : (n + 2) * each].astype(jnp.bfloat16)

    return emit


def beams_of(ref, first, count):
    return [(ref, first + b) for b in range(count)]


def own_part_kernel(count, params, rtab, mine, other, spec, lags, dops, r_ref, part_ref, padded, prods, corrs):
    write_ref_spectra(params, rtab, mine, other, r_ref, padded)

    def emit(k, power):
        part_ref[k] = power

    sum_powers([(beams_of(spec, 0, count), r_ref)], lags, dops, prods, corrs, emit)


def far_part_kernel(
    count, params, rtab, mine, other, stab, s_ref, part_ref, lags, dops, r_ref, far_spec, own_ref, *refs
):
    send_refs, (padded, prods, corrs) = refs[:-3], refs[-3:]
    write_ref_spectra(params, rtab, mine, other, r_ref, padded)
    surv_spectra_kernel(stab, s_ref, far_spec)
    store = emit_chunks(own_ref, send_refs)
    emit = lambda k, power: store(k, power + part_ref[k])
    sum_powers([(beams_of(far_spec, 0, count), r_ref)], lags, dops, prods, corrs, emit)


def both_kernel(first, count, spec, far_spec, r_here, r_there, lags, dops, own_ref, *refs):
    send_refs, (prods, corrs) = refs[:-2], refs[-2:]
    emit = emit_chunks(own_ref, send_refs)
    segments = [(beams_of(s, first, count), r) for s, r in ((spec, r_here), (far_spec, r_there))]
    sum_powers(segments, lags, dops, prods, corrs, emit)


def assemble_kernel(n_seg, sizes, params, *refs):
    out_ref = refs[-1]
    groups = [refs[g * n_seg : (g + 1) * n_seg] for g in range(len(sizes))]
    half = out_ref.shape[1] // 2
    part = params[2 * TX + 1] % 2

    def total(refs, k):
        return functools.reduce(jnp.add, [r[k].astype(jnp.float32) for r in refs]) * (1.0 / n_seg)

    for k in range(TX):
        first = 0
        for size, group in zip(sizes, groups, strict=True):
            out_ref[k, pl.ds(part * half + first, size)] = total(group[::2], k)
            out_ref[k, pl.ds((1 - part) * half + first, size)] = total(group[1::2], k)
            first += size


def call_powers(kernel, name, args, out_shape, count, segments, ref_spectra):
    padded = pltpu.VMEM((BLOCKS + 2 * PAD, PAIR), jnp.float32)
    work = [
        pltpu.VMEM((segments, 2 * FFT, count * BLOCKS), jnp.bfloat16),
        pltpu.VMEM((2, segments * count * DELAYS, 2 * BLOCKS), jnp.bfloat16),
    ]
    return pl.pallas_call(
        kernel,
        in_specs=[SMEM if a.ndim == 1 else VMEM for a in args],
        out_specs=[VMEM] * len(out_shape),
        out_shape=out_shape,
        scratch_shapes=[padded] * ref_spectra + work,
        compiler_params=pltpu.CompilerParams(vmem_limit_bytes=VMEM_LIMIT),
        cost_estimate=pl.CostEstimate(
            flops=segments * count * TX * 2 * 768 * 65536, bytes_accessed=6 << 20, transcendentals=0
        ),
        name=name,
    )(*args)


def swap(value, axis, flip):
    size = lax.axis_size(axis)
    return lax.ppermute(value, axis, [(i, i ^ flip) for i in range(size)])


def shards(voltages, surv_taps, ref_taps, tx_owner, delay_start, doppler_start):
    beams_here = voltages.shape[1]
    n_beam = lax.axis_size("beam")
    n_seg = lax.axis_size("seg")
    ids = jnp.stack([lax.axis_index("beam"), lax.axis_index("seg")]).astype(jnp.int32)
    volts = voltages.reshape(2, beams_here, voltages.shape[3])
    out = decimate(
        volts,
        surv_taps.reshape(1, TAPS),
        ref_taps.reshape(1, TAPS),
        ids,
        tx_owner,
        delay_start,
        doppler_start,
    )
    here, give, keep, send, params = out
    stab, rtab = jnp.asarray(surv_fourier()), jnp.asarray(ref_fourier())
    there = swap(give, "seg", 1)
    half = keep + swap(send, "beam", 1)
    half, here, params = lax.optimization_barrier((half, here, params))
    got = [swap(half, "beam", flip) for flip in range(2, n_beam, 2)]
    lags, dops = make_tables(params, n_seg)
    spec = surv_spectra(stab, here, "own_spectra")
    got, lags, dops, spec = lax.optimization_barrier((got, lags, dops, spec))
    half = functools.reduce(jnp.add, got, half)
    other = swap(half, "beam", 1)
    far = swap(half, "seg", 1)
    leaving, there = lax.optimization_barrier((other, there))
    far_other = swap(leaving, "seg", 1)

    each = DELAYS // n_seg
    r_shape = jax.ShapeDtypeStruct((TX, 2 * FFT, BLOCKS), jnp.float32)
    chunks = lambda n: [jax.ShapeDtypeStruct((TX, n, each, DOPPLER), jnp.float32)] + [
        jax.ShapeDtypeStruct((TX, n, each, DOPPLER), jnp.bfloat16)
    ] * (n_seg - 1)
    sizes = [n * beams_here // 16 for n in GROUPS]
    count = sizes[0]
    r_here, part = call_powers(
        functools.partial(own_part_kernel, count),
        "own_part",
        (params, rtab, half, other, spec, lags, dops),
        [r_shape, jax.ShapeDtypeStruct((TX, count, DELAYS, DOPPLER), jnp.float32)],
        count,
        1,
        True,
    )
    behind = []
    collected = []
    first = 0
    for g, count in enumerate(sizes):
        if g == 0:
            r_there, far_spec, own, *sends = call_powers(
                functools.partial(far_part_kernel, count),
                "far_part",
                (params, rtab, far, far_other, stab, there, part, lags, dops),
                [r_shape, jax.ShapeDtypeStruct(spec.shape, spec.dtype)] + chunks(count),
                count,
                1,
                True,
            )
        else:
            own, *sends = call_powers(
                functools.partial(both_kernel, first, count),
                "both",
                (spec, far_spec, r_here, r_there, lags, dops),
                chunks(count),
                count,
                2,
                False,
            )
        sends[0], *behind = lax.optimization_barrier((sends[0], *behind))
        arrived = [swap(s, "seg", n + 1) for n, s in enumerate(sends)]
        collected += [own] + arrived
        behind = arrived[1:]
        first += count
    return pl.pallas_call(
        functools.partial(assemble_kernel, n_seg, sizes),
        in_specs=[SMEM] + [VMEM] * len(collected),
        out_specs=VMEM,
        out_shape=jax.ShapeDtypeStruct((TX, beams_here, each, DOPPLER), jnp.float32),
        compiler_params=pltpu.CompilerParams(vmem_limit_bytes=VMEM_LIMIT),
        name="assemble",
    )(params, *collected)


def solution(mesh):
    return jax.shard_map(
        shards,
        mesh=mesh,
        in_specs=(P(None, "beam", "seg", None), P(), P(), P(), P(), P()),
        out_specs=P(None, "beam", "seg", None),
        check_vma=False,
    )
```

```python
import functools

import jax
import jax.numpy as jnp
import ml_dtypes
import numpy as np
from jax import lax
from jax.experimental import pallas as pl
from jax.experimental.pallas import tpu as pltpu
from jax.sharding import PartitionSpec as P

TX = 4
HALF_TX = TX // 2
DECIM = 4
TAPS = 32
BLOCK_LEN = 64
BLOCKS = 256
DELAYS = 128
DOPPLER = 128
FFT = 256
STRIDE = DECIM * BLOCK_LEN
LEAD = 128
REACH = LEAD + STRIDE
PAIR = 2 * BLOCK_LEN
TOGETHER = 4
LANES = 128
LANE_BLOCKS = 2 * FFT // LANES
VMEM_LIMIT = 24 * 1024 * 1024
OWN_FLOPS = 1_600_000_000
FAR_FLOPS = 1_600_000_000
BOTH_FLOPS = 3_200_000_000

SMEM = pl.BlockSpec(memory_space=pltpu.SMEM)
VMEM = pl.BlockSpec(memory_space=pltpu.VMEM)
HBM = pl.BlockSpec(memory_space=pltpu.HBM)


def split_bf16(table):
    hi = table.astype(ml_dtypes.bfloat16)
    lo = (table - hi.astype(np.float64)).astype(ml_dtypes.bfloat16)
    return hi, lo


def fourier(samples):
    angle = 2 * np.pi / FFT * (np.outer(np.arange(FFT), samples) % FFT)
    cos, sin = np.cos(angle), np.sin(angle)
    return np.block([[cos, sin], [-sin, cos]])


def surv_fourier():
    hi, lo = split_bf16(fourier(np.arange(BLOCK_LEN)))
    return np.concatenate([hi, lo], axis=1)


def ref_fourier():
    parts = [fourier(np.arange(BLOCK_LEN) + BLOCK_LEN * e) for e in range(4)]
    hi, lo = split_bf16(np.concatenate(parts, axis=1))
    return np.concatenate([hi, lo], axis=1)


def in_lane_blocks(both):
    parts, rows, _ = both.shape
    return both.astype(np.float32).reshape(parts, rows, LANE_BLOCKS, LANES).swapaxes(1, 2)


def lag_table():
    lags = 191 - np.arange(192)
    angle = 2 * np.pi / FFT * (np.outer(lags, np.arange(FFT)) % FFT)
    cos, sin = np.cos(angle), np.sin(angle)
    scale = 1.0 / (FFT * np.sqrt(BLOCK_LEN))
    both = np.stack([np.concatenate([cos, sin], 1), np.concatenate([-sin, cos], 1)])
    both = both.astype(ml_dtypes.bfloat16).astype(np.float64) * scale
    return in_lane_blocks(both)


def doppler_table():
    freqs = np.arange(BLOCKS) - BLOCKS // 2
    angle = 2 * np.pi / BLOCKS * (np.outer(freqs, np.arange(BLOCKS)) % BLOCKS)
    cos, sin = np.cos(angle), np.sin(angle)
    both = np.stack([np.concatenate([cos, sin], 1), np.concatenate([-sin, cos], 1)])
    return in_lane_blocks(both.astype(ml_dtypes.bfloat16))


def nt_dot(left, right):
    return lax.dot_general(
        left, right, (((1,), (1,)), ((), ())), preferred_element_type=jnp.float32
    )


def dot(left, right):
    return jnp.dot(left, right, preferred_element_type=jnp.float32)


def decimate_kernel(beams, ids, owner, delay, doppler, staps, rtaps, volts, *refs):
    here_ref, give_ref, keep_ref, send_ref, params, x, taps, small, band, all_s, all_r, sems, small_sems = refs
    chunks = sems.shape[0]
    raw = volts.shape[2]
    wide = raw // chunks
    rows = wide // STRIDE
    blocks = raw // STRIDE
    smalls = [
        pltpu.make_async_copy(ref, small.at[n], small_sems.at[n])
        for n, ref in enumerate((owner, delay, doppler))
    ]
    smalls += [
        pltpu.make_async_copy(ref, taps.at[n], small_sems.at[3 + n])
        for n, ref in enumerate((staps, rtaps))
    ]
    copies = [
        pltpu.make_async_copy(
            volts.at[:, :, pl.ds(n * wide, wide)],
            x.at[:, :, pl.ds(LEAD + n * wide, wide)],
            sems.at[n],
        )
        for n in range(chunks)
    ]
    for copy in smalls + copies:
        copy.start()
    x[:, :, :LEAD] = jnp.zeros((2, beams, LEAD), jnp.bfloat16)
    for copy in smalls:
        copy.wait()

    shape = (REACH, PAIR)
    q = lax.broadcasted_iota(jnp.int32, shape, 0)
    lane = lax.broadcasted_iota(jnp.int32, shape, 1)
    tap = LEAD + DECIM * (lane % BLOCK_LEN) - q
    first = lane < BLOCK_LEN
    one, two = taps[0].astype(jnp.float32), taps[1].astype(jnp.float32)
    both = jnp.zeros(shape, jnp.float32)
    for t in range(TAPS):
        row = jnp.where(first[:1], one[:, t : t + 1], two[:, t : t + 1])
        both = jnp.where(tap == t, row, both)
    turned = pltpu.roll(both, BLOCK_LEN, 1)
    zero = jnp.zeros(shape, jnp.float32)
    band[:REACH, :PAIR] = jnp.where(first, both, zero).astype(jnp.bfloat16)
    band[REACH:, :PAIR] = jnp.where(first, zero, turned).astype(jnp.bfloat16)
    band[:REACH, PAIR:] = jnp.where(first, turned, zero).astype(jnp.bfloat16)
    band[REACH:, PAIR:] = jnp.where(first, zero, both).astype(jnp.bfloat16)
    for k in range(TX):
        params[k] = small[1, k]
        params[TX + k] = small[2, k]
    params[2 * TX] = ids[0]
    params[2 * TX + 1] = ids[1]

    def step(n, _):
        pltpu.make_async_copy(
            volts.at[:, :, pl.ds(n * wide, wide)],
            x.at[:, :, pl.ds(LEAD + n * wide, wide)],
            sems.at[n],
        ).wait()
        parts = []
        for c in range(2):
            starts = [pl.multiple_of(n * wide + l * STRIDE, STRIDE) for l in range(rows)]
            parts.append(jnp.concatenate([x[c, :, pl.ds(at, REACH)] for at in starts], axis=0))
        out = dot(jnp.concatenate(parts, axis=1), band[...])
        span = pl.ds(pl.multiple_of(n * rows * beams, rows * beams), rows * beams)
        all_s[span] = out[:, :PAIR]
        all_r[span] = out[:, PAIR:]
        here = pl.ds(pl.multiple_of(n * rows, rows), rows)
        part = ids[1] % 2
        half = beams // 2
        for s_ref, at in ((here_ref, part * half), (give_ref, (1 - part) * half)):
            for b in range(half):
                picked = all_s[pl.ds(n * rows * beams + at + b, rows, stride=beams), :]
                s_ref[b, here] = picked.astype(jnp.bfloat16)
        return 0

    lax.fori_loop(0, chunks, step, 0)
    core = ids[0] % 2
    for ref, first_tx in ((keep_ref, core * HALF_TX), (send_ref, (1 - core) * HALF_TX)):
        for k in range(HALF_TX):
            beam = small[0, first_tx + k]
            picked = all_r[pl.ds(beam % beams, blocks, stride=beams), :]
            ref[k] = jnp.where(beam // beams == ids[0], picked, 0.0).astype(jnp.bfloat16)


def decimate(volts, staps, rtaps, ids, owner, delay, doppler):
    beams, raw = volts.shape[1:]
    blocks = raw // STRIDE
    chunks = 1
    arrays = (owner, delay, doppler, staps, rtaps, volts)
    shape = lambda n: jax.ShapeDtypeStruct((n, blocks, PAIR), jnp.bfloat16)
    return pl.pallas_call(
        functools.partial(decimate_kernel, beams),
        in_specs=[SMEM] + [HBM] * 6,
        out_specs=[VMEM] * 4 + [SMEM],
        out_shape=[shape(beams // 2)] * 2
        + [shape(HALF_TX)] * 2
        + [jax.ShapeDtypeStruct((2 * TX + 2,), jnp.int32)],
        scratch_shapes=[
            pltpu.VMEM((2, beams, LEAD + raw), jnp.bfloat16),
            pltpu.VMEM((2, 1, TAPS), jnp.bfloat16),
            pltpu.SMEM((3, TX), jnp.int32),
            pltpu.VMEM((2 * REACH, 2 * PAIR), jnp.bfloat16),
            pltpu.VMEM((blocks * beams, PAIR), jnp.float32),
            pltpu.VMEM((blocks * beams, PAIR), jnp.float32),
            pltpu.SemaphoreType.DMA((chunks,)),
            pltpu.SemaphoreType.DMA((5,)),
        ],
        compiler_params=pltpu.CompilerParams(vmem_limit_bytes=VMEM_LIMIT),
        name="decimate",
    )(ids, *(pltpu.with_memory_space_constraint(a, pltpu.HBM) for a in arrays))


def tables_kernel(chunks, params, lag_ref, dop_ref, lags, dops):
    each = DELAYS // chunks
    for k in range(TX):
        base = (params[k] + DELAYS - 1) % BLOCK_LEN
        for part in range(2):
            for n in range(chunks):
                chunk = params[2 * TX + 1] ^ n
                at = part * DELAYS + n * each
                for q in range(LANE_BLOCKS):
                    picked = lag_ref[part, q, pl.ds(base + chunk * each, each), :]
                    lags[k, at : at + each, q * LANES : (q + 1) * LANES] = picked.astype(jnp.bfloat16)
            for q in range(LANE_BLOCKS):
                picked = dop_ref[part, q, pl.ds(params[TX + k], DOPPLER), :].T.astype(jnp.bfloat16)
                dops[k, q * LANES : (q + 1) * LANES, part * DOPPLER : (part + 1) * DOPPLER] = picked


def make_tables(params, chunks):
    return pl.pallas_call(
        functools.partial(tables_kernel, chunks),
        in_specs=[SMEM, VMEM, VMEM],
        out_specs=[VMEM, VMEM],
        out_shape=[
            jax.ShapeDtypeStruct((TX, 2 * DELAYS, 2 * FFT), jnp.bfloat16),
            jax.ShapeDtypeStruct((TX, 2 * BLOCKS, 2 * DOPPLER), jnp.bfloat16),
        ],
        compiler_params=pltpu.CompilerParams(vmem_limit_bytes=VMEM_LIMIT),
        name="tables",
    )(params, jnp.asarray(lag_table()), jnp.asarray(doppler_table()))


PAD = 8


def first_tx(params, group):
    core = params[2 * TX] % 2
    return (core if group == 0 else 1 - core) * HALF_TX


def write_ref_spectra(params, first, table_ref, ref, out_ref, padded):
    padded[:PAD] = jnp.zeros((PAD, PAIR), jnp.float32)
    padded[PAD + BLOCKS :] = jnp.zeros((PAD, PAIR), jnp.float32)
    for k in range(HALF_TX):
        padded[PAD : PAD + BLOCKS] = ref[k].astype(jnp.float32)
        start = PAD - 1 - (params[first + k] + DELAYS - 1) // BLOCK_LEN
        window = jnp.concatenate(
            [padded[pl.ds(start + e, BLOCKS), :].astype(jnp.bfloat16) for e in range(4)], axis=1
        )
        out_ref[k] = nt_dot(table_ref[...], jnp.concatenate([window, window], axis=1))


def surv_spectrum(table_ref, s):
    return nt_dot(table_ref[...], jnp.concatenate([s, s], axis=1))


def surv_spectra_kernel(table_ref, s_ref, out_ref):
    for b in range(s_ref.shape[0]):
        out_ref[b] = surv_spectrum(table_ref, s_ref[b])


def surv_spectra(table, surv, name):
    return pl.pallas_call(
        surv_spectra_kernel,
        in_specs=[VMEM] * 2,
        out_specs=VMEM,
        out_shape=jax.ShapeDtypeStruct((surv.shape[0], 2 * FFT, BLOCKS), jnp.float32),
        compiler_params=pltpu.CompilerParams(vmem_limit_bytes=VMEM_LIMIT),
        name=name,
    )(table, surv)


def sum_powers(segments, first, lag_ref, dop_ref, prods, corrs, emit):
    count = segments[0][0].shape[0]
    rows = count * DELAYS
    for k in range(HALF_TX):
        corr = corrs.at[k]
        for n, (s_ref, r_ref) in enumerate(segments):
            r_re, r_im = r_ref[k, :FFT], r_ref[k, FFT:]
            prod = prods.at[n]
            for b in range(count):
                cols = slice(b * BLOCKS, (b + 1) * BLOCKS)
                s_re, s_im = s_ref[b, :FFT], s_ref[b, FFT:]
                prod[:FFT, cols] = (s_re * r_re + s_im * r_im).astype(jnp.bfloat16)
                prod[FFT:, cols] = (s_im * r_re - s_re * r_im).astype(jnp.bfloat16)
            out = dot(lag_ref[first + k], prod[...]).astype(jnp.bfloat16)
            for b in range(count):
                cols = slice(b * BLOCKS, (b + 1) * BLOCKS)
                at = n * rows + b * DELAYS
                corr[at : at + DELAYS, :BLOCKS] = out[:DELAYS, cols]
                corr[at : at + DELAYS, BLOCKS:] = out[DELAYS:, cols]
        for b in range(0, count, TOGETHER):
            power = 0.0
            for n in range(len(segments)):
                at = n * rows + b * DELAYS
                x = dot(corr[at : at + TOGETHER * DELAYS], dop_ref[first + k])
                x_re, x_im = x[:, :DOPPLER], x[:, DOPPLER:]
                power = power + (x_re * x_re + x_im * x_im) * (1.0 / (4 * BLOCKS))
            emit(k, slice(b, b + TOGETHER), power.reshape(TOGETHER, DELAYS, DOPPLER))


def emit_chunks(own_ref, send_refs):
    each = own_ref.shape[2]

    def emit(k, at, power):
        own_ref[k, at] = power[:, :each]
        for n, ref in enumerate(send_refs):
            ref[k, at] = power[:, (n + 1) * each : (n + 2) * each].astype(jnp.bfloat16)

    return emit


def own_part_kernel(params, rtab, mine, spec, lags, dops, part_ref, padded, r_here, prods, corrs):
    first = first_tx(params, 0)
    write_ref_spectra(params, first, rtab, mine, r_here, padded)

    def emit(k, at, power):
        part_ref[k, at] = power

    sum_powers([(spec, r_here)], first, lags, dops, prods, corrs, emit)


def far_part_kernel(params, rtab, far, stab, there, part_ref, lags, dops, far_spec, own_ref, *refs):
    send_refs, (padded, r_there, prods, corrs) = refs[:-4], refs[-4:]
    first = first_tx(params, 0)
    write_ref_spectra(params, first, rtab, far, r_there, padded)
    surv_spectra_kernel(stab, there, far_spec)
    store = emit_chunks(own_ref, send_refs)
    emit = lambda k, at, power: store(k, at, power + part_ref[k, at])
    sum_powers([(far_spec, r_there)], first, lags, dops, prods, corrs, emit)


def both_kernel(
    params, rtab, mine, far, spec, far_spec, near_ref, lags, dops, own_ref, near_all, *refs
):
    send_refs, (padded, r_here, r_there, prods, corrs) = refs[:-5], refs[-5:]
    first = first_tx(params, 1)
    write_ref_spectra(params, first, rtab, mine, r_here, padded)
    write_ref_spectra(params, first, rtab, far, r_there, padded)
    near_all[:HALF_TX] = near_ref[...]
    emit = emit_chunks(own_ref, (near_all.at[HALF_TX:], *send_refs))
    sum_powers([(spec, r_here), (far_spec, r_there)], first, lags, dops, prods, corrs, emit)


def assemble_kernel(n_seg, params, near_ref, *refs):
    groups, (out_ref, mean, sems) = refs[:-3], refs[-3:]
    half = out_ref.shape[1] // 2
    part = params[2 * TX + 1] % 2

    def total(values):
        return functools.reduce(jnp.add, [v.astype(jnp.float32) for v in values]) * (1.0 / n_seg)

    copies = []
    for g in range(2):
        own, *arrived = groups[g * (n_seg - 1) : (g + 1) * (n_seg - 1)]
        for k in range(HALF_TX):
            at = g * HALF_TX + k
            mean[at, pl.ds(part * half, half)] = total([r[k] for r in (own, *arrived[0::2])])
            theirs = total([near_ref[at]] + [r[k] for r in arrived[1::2]])
            mean[at, pl.ds((1 - part) * half, half)] = theirs
            copy = pltpu.make_async_copy(
                mean.at[at], out_ref.at[first_tx(params, g) + k], sems.at[at]
            )
            copy.start()
            copies.append(copy)
    for copy in copies:
        copy.wait()


def call_powers(kernel, name, args, out_shape, count, segments, flops):
    return pl.pallas_call(
        kernel,
        in_specs=[SMEM if a.ndim == 1 else VMEM for a in args],
        out_specs=[VMEM] * len(out_shape),
        out_shape=out_shape,
        scratch_shapes=[pltpu.VMEM((BLOCKS + 2 * PAD, PAIR), jnp.float32)]
        + [pltpu.VMEM((HALF_TX, 2 * FFT, BLOCKS), jnp.float32)] * segments
        + [
            pltpu.VMEM((segments, 2 * FFT, count * BLOCKS), jnp.bfloat16),
            pltpu.VMEM((HALF_TX, segments * count * DELAYS, 2 * BLOCKS), jnp.bfloat16),
        ],
        compiler_params=pltpu.CompilerParams(vmem_limit_bytes=VMEM_LIMIT * count // 8),
        cost_estimate=pl.CostEstimate(flops=flops, bytes_accessed=1 << 20, transcendentals=0),
        name=name,
    )(*args)


def swap(value, axis, flip):
    size = lax.axis_size(axis)
    return lax.ppermute(value, axis, [(i, i ^ flip) for i in range(size)])


def shards(voltages, surv_taps, ref_taps, tx_owner, delay_start, doppler_start):
    beams_here = voltages.shape[1]
    n_beam = lax.axis_size("beam")
    n_seg = lax.axis_size("seg")
    ids = jnp.stack([lax.axis_index("beam"), lax.axis_index("seg")]).astype(jnp.int32)
    volts = voltages.reshape(2, beams_here, voltages.shape[3])
    out = decimate(
        volts,
        surv_taps.reshape(1, TAPS),
        ref_taps.reshape(1, TAPS),
        ids,
        tx_owner,
        delay_start,
        doppler_start,
    )
    here, give, keep, send, params = out
    stab, rtab = jnp.asarray(surv_fourier()), jnp.asarray(ref_fourier())
    there = swap(give, "seg", 1)
    half = keep + swap(send, "beam", 1)
    half, here, params = lax.optimization_barrier((half, here, params))
    got = [swap(half, "beam", flip) for flip in range(2, n_beam, 2)]
    lags, dops = make_tables(params, n_seg)
    spec = surv_spectra(stab, here, "own_spectra")
    got, lags, dops, spec = lax.optimization_barrier((got, lags, dops, spec))
    half = functools.reduce(jnp.add, got, half)
    other = swap(half, "beam", 1)
    far = swap(half, "seg", 1)
    far_other = swap(other, "seg", 1)
    spec, there = lax.optimization_barrier((spec, there))
    count = beams_here // 2
    each = DELAYS // n_seg
    kept = lambda n: jax.ShapeDtypeStruct((HALF_TX, count, n, DOPPLER), jnp.float32)
    sent = lambda n: jax.ShapeDtypeStruct((n, count, each, DOPPLER), jnp.bfloat16)
    (part,) = call_powers(
        own_part_kernel,
        "own_part",
        (params, rtab, half, spec, lags, dops),
        [kept(DELAYS)],
        count,
        1,
        OWN_FLOPS,
    )
    far_spec, own, near, *long_way = call_powers(
        far_part_kernel,
        "far_part",
        (params, rtab, far, stab, there, part, lags, dops),
        [jax.ShapeDtypeStruct(spec.shape, spec.dtype), kept(each)] + [sent(HALF_TX)] * (n_seg - 1),
        count,
        1,
        FAR_FLOPS,
    )
    arrived = [swap(s, "seg", n) for n, s in enumerate(long_way, 2)]
    collected = [own] + arrived
    own, near, *long_way = call_powers(
        both_kernel,
        "both",
        (params, rtab, other, far_other, spec, far_spec, near, lags, dops),
        [kept(each), sent(TX)] + [sent(HALF_TX)] * (n_seg - 2),
        count,
        2,
        BOTH_FLOPS,
    )
    near = swap(near, "seg", 1)
    long_way[-1], *arrived = lax.optimization_barrier((long_way[-1], *arrived))
    collected += [own] + [swap(s, "seg", n) for n, s in enumerate(long_way, 2)]
    out = (TX, beams_here, each, DOPPLER)
    return pl.pallas_call(
        functools.partial(assemble_kernel, n_seg),
        in_specs=[SMEM] + [VMEM] * (1 + len(collected)),
        out_specs=pl.BlockSpec(memory_space=pl.ANY),
        out_shape=jax.ShapeDtypeStruct(out, jnp.float32),
        scratch_shapes=[pltpu.VMEM(out, jnp.float32), pltpu.SemaphoreType.DMA((TX,))],
        compiler_params=pltpu.CompilerParams(vmem_limit_bytes=VMEM_LIMIT),
        name="assemble",
    )(params, near, *collected)


def solution(mesh):
    return jax.shard_map(
        shards,
        mesh=mesh,
        in_specs=(P(None, "beam", "seg", None), P(), P(), P(), P(), P()),
        out_specs=P(None, "beam", "seg", None),
        check_vma=False,
    )
```

```python
import functools

import jax
import jax.numpy as jnp
import ml_dtypes
import numpy as np
from jax import lax
from jax.experimental import pallas as pl
from jax.experimental.pallas import tpu as pltpu
from jax.sharding import PartitionSpec as P

TX = 4
HALF_TX = TX // 2
DECIM = 4
TAPS = 32
BLOCK_LEN = 64
BLOCKS = 256
DELAYS = 128
DOPPLER = 128
FFT = 256
STRIDE = DECIM * BLOCK_LEN
LEAD = 128
REACH = LEAD + STRIDE
PAIR = 2 * BLOCK_LEN
TOGETHER = 4
LANES = 128
LANE_BLOCKS = 2 * FFT // LANES
VMEM_LIMIT = 24 * 1024 * 1024
OWN_FLOPS = 1_600_000_000
FAR_FLOPS = 1_600_000_000
BOTH_FLOPS = 3_200_000_000

SMEM = pl.BlockSpec(memory_space=pltpu.SMEM)
VMEM = pl.BlockSpec(memory_space=pltpu.VMEM)
HBM = pl.BlockSpec(memory_space=pltpu.HBM)


def split_bf16(table):
    hi = table.astype(ml_dtypes.bfloat16)
    lo = (table - hi.astype(np.float64)).astype(ml_dtypes.bfloat16)
    return hi, lo


def fourier(samples):
    angle = 2 * np.pi / FFT * (np.outer(np.arange(FFT), samples) % FFT)
    cos, sin = np.cos(angle), np.sin(angle)
    return np.block([[cos, sin], [-sin, cos]])


def surv_fourier():
    hi, lo = split_bf16(fourier(np.arange(BLOCK_LEN)))
    return np.concatenate([hi, lo], axis=1)


def ref_fourier():
    parts = [fourier(np.arange(BLOCK_LEN) + BLOCK_LEN * e) for e in range(4)]
    hi, lo = split_bf16(np.concatenate(parts, axis=1))
    return np.concatenate([hi, lo], axis=1)


def in_lane_blocks(both):
    parts, rows, _ = both.shape
    return both.astype(np.float32).reshape(parts, rows, LANE_BLOCKS, LANES).swapaxes(1, 2)


def lag_table():
    lags = 191 - np.arange(192)
    angle = 2 * np.pi / FFT * (np.outer(lags, np.arange(FFT)) % FFT)
    cos, sin = np.cos(angle), np.sin(angle)
    scale = 1.0 / (FFT * np.sqrt(BLOCK_LEN))
    both = np.stack([np.concatenate([cos, sin], 1), np.concatenate([-sin, cos], 1)])
    both = both.astype(ml_dtypes.bfloat16).astype(np.float64) * scale
    return in_lane_blocks(both)


def doppler_table():
    freqs = np.arange(BLOCKS) - BLOCKS // 2
    angle = 2 * np.pi / BLOCKS * (np.outer(freqs, np.arange(BLOCKS)) % BLOCKS)
    cos, sin = np.cos(angle), np.sin(angle)
    both = np.stack([np.concatenate([cos, sin], 1), np.concatenate([-sin, cos], 1)])
    return in_lane_blocks(both.astype(ml_dtypes.bfloat16))


def nt_dot(left, right):
    return lax.dot_general(
        left, right, (((1,), (1,)), ((), ())), preferred_element_type=jnp.float32
    )


def dot(left, right):
    return jnp.dot(left, right, preferred_element_type=jnp.float32)


def decimate_kernel(beams, ids, owner, delay, doppler, staps, rtaps, volts, *refs):
    here_ref, give_ref, keep_ref, send_ref, params, x, taps, small, band, all_s, all_r, sems, small_sems = refs
    chunks = sems.shape[0]
    raw = volts.shape[2]
    wide = raw // chunks
    rows = wide // STRIDE
    blocks = raw // STRIDE
    smalls = [
        pltpu.make_async_copy(ref, small.at[n], small_sems.at[n])
        for n, ref in enumerate((owner, delay, doppler))
    ]
    smalls += [
        pltpu.make_async_copy(ref, taps.at[n], small_sems.at[3 + n])
        for n, ref in enumerate((staps, rtaps))
    ]
    copies = [
        pltpu.make_async_copy(
            volts.at[:, :, pl.ds(n * wide, wide)],
            x.at[:, :, pl.ds(LEAD + n * wide, wide)],
            sems.at[n],
        )
        for n in range(chunks)
    ]
    for copy in smalls + copies:
        copy.start()
    x[:, :, :LEAD] = jnp.zeros((2, beams, LEAD), jnp.bfloat16)
    for copy in smalls:
        copy.wait()

    shape = (REACH, PAIR)
    q = lax.broadcasted_iota(jnp.int32, shape, 0)
    lane = lax.broadcasted_iota(jnp.int32, shape, 1)
    tap = LEAD + DECIM * (lane % BLOCK_LEN) - q
    first = lane < BLOCK_LEN
    one, two = taps[0].astype(jnp.float32), taps[1].astype(jnp.float32)
    both = jnp.zeros(shape, jnp.float32)
    for t in range(TAPS):
        row = jnp.where(first[:1], one[:, t : t + 1], two[:, t : t + 1])
        both = jnp.where(tap == t, row, both)
    turned = pltpu.roll(both, BLOCK_LEN, 1)
    zero = jnp.zeros(shape, jnp.float32)
    band[:REACH, :PAIR] = jnp.where(first, both, zero).astype(jnp.bfloat16)
    band[REACH:, :PAIR] = jnp.where(first, zero, turned).astype(jnp.bfloat16)
    band[:REACH, PAIR:] = jnp.where(first, turned, zero).astype(jnp.bfloat16)
    band[REACH:, PAIR:] = jnp.where(first, zero, both).astype(jnp.bfloat16)
    for k in range(TX):
        params[k] = small[1, k]
        params[TX + k] = small[2, k]
    params[2 * TX] = ids[0]
    params[2 * TX + 1] = ids[1]

    def step(n, _):
        pltpu.make_async_copy(
            volts.at[:, :, pl.ds(n * wide, wide)],
            x.at[:, :, pl.ds(LEAD + n * wide, wide)],
            sems.at[n],
        ).wait()
        parts = []
        for c in range(2):
            starts = [pl.multiple_of(n * wide + l * STRIDE, STRIDE) for l in range(rows)]
            parts.append(jnp.concatenate([x[c, :, pl.ds(at, REACH)] for at in starts], axis=0))
        out = dot(jnp.concatenate(parts, axis=1), band[...])
        span = pl.ds(pl.multiple_of(n * rows * beams, rows * beams), rows * beams)
        all_s[span] = out[:, :PAIR]
        all_r[span] = out[:, PAIR:]
        here = pl.ds(pl.multiple_of(n * rows, rows), rows)
        part = ids[1] % 2
        half = beams // 2
        for s_ref, at in ((here_ref, part * half), (give_ref, (1 - part) * half)):
            for b in range(half):
                picked = all_s[pl.ds(n * rows * beams + at + b, rows, stride=beams), :]
                s_ref[b, here] = picked.astype(jnp.bfloat16)
        return 0

    lax.fori_loop(0, chunks, step, 0)
    core = ids[0] % 2
    for ref, first_tx in ((keep_ref, core * HALF_TX), (send_ref, (1 - core) * HALF_TX)):
        for k in range(HALF_TX):
            beam = small[0, first_tx + k]
            picked = all_r[pl.ds(beam % beams, blocks, stride=beams), :]
            ref[k] = jnp.where(beam // beams == ids[0], picked, 0.0).astype(jnp.bfloat16)


def decimate(volts, staps, rtaps, ids, owner, delay, doppler):
    beams, raw = volts.shape[1:]
    blocks = raw // STRIDE
    chunks = 1
    arrays = (owner, delay, doppler, staps, rtaps, volts)
    shape = lambda n: jax.ShapeDtypeStruct((n, blocks, PAIR), jnp.bfloat16)
    return pl.pallas_call(
        functools.partial(decimate_kernel, beams),
        in_specs=[SMEM] + [HBM] * 6,
        out_specs=[VMEM] * 4 + [SMEM],
        out_shape=[shape(beams // 2)] * 2
        + [shape(HALF_TX)] * 2
        + [jax.ShapeDtypeStruct((2 * TX + 2,), jnp.int32)],
        scratch_shapes=[
            pltpu.VMEM((2, beams, LEAD + raw), jnp.bfloat16),
            pltpu.VMEM((2, 1, TAPS), jnp.bfloat16),
            pltpu.SMEM((3, TX), jnp.int32),
            pltpu.VMEM((2 * REACH, 2 * PAIR), jnp.bfloat16),
            pltpu.VMEM((blocks * beams, PAIR), jnp.float32),
            pltpu.VMEM((blocks * beams, PAIR), jnp.float32),
            pltpu.SemaphoreType.DMA((chunks,)),
            pltpu.SemaphoreType.DMA((5,)),
        ],
        compiler_params=pltpu.CompilerParams(vmem_limit_bytes=VMEM_LIMIT),
        name="decimate",
    )(ids, *(pltpu.with_memory_space_constraint(a, pltpu.HBM) for a in arrays))


def tables_kernel(chunks, params, lag_ref, dop_ref, lags, dops):
    each = DELAYS // chunks
    for k in range(TX):
        base = (params[k] + DELAYS - 1) % BLOCK_LEN
        for part in range(2):
            for n in range(chunks):
                chunk = params[2 * TX + 1] ^ n
                at = part * DELAYS + n * each
                for q in range(LANE_BLOCKS):
                    picked = lag_ref[part, q, pl.ds(base + chunk * each, each), :]
                    lags[k, at : at + each, q * LANES : (q + 1) * LANES] = picked.astype(jnp.bfloat16)
            for q in range(LANE_BLOCKS):
                picked = dop_ref[part, q, pl.ds(params[TX + k], DOPPLER), :].T.astype(jnp.bfloat16)
                dops[k, q * LANES : (q + 1) * LANES, part * DOPPLER : (part + 1) * DOPPLER] = picked


def make_tables(params, chunks):
    return pl.pallas_call(
        functools.partial(tables_kernel, chunks),
        in_specs=[SMEM, VMEM, VMEM],
        out_specs=[VMEM, VMEM],
        out_shape=[
            jax.ShapeDtypeStruct((TX, 2 * DELAYS, 2 * FFT), jnp.bfloat16),
            jax.ShapeDtypeStruct((TX, 2 * BLOCKS, 2 * DOPPLER), jnp.bfloat16),
        ],
        compiler_params=pltpu.CompilerParams(vmem_limit_bytes=VMEM_LIMIT),
        name="tables",
    )(params, jnp.asarray(lag_table()), jnp.asarray(doppler_table()))


PAD = 8


def first_tx(params, group):
    core = params[2 * TX] % 2
    return (core if group == 0 else 1 - core) * HALF_TX


def write_ref_spectra(params, first, table_ref, ref, out_ref, padded):
    padded[:PAD] = jnp.zeros((PAD, PAIR), jnp.float32)
    padded[PAD + BLOCKS :] = jnp.zeros((PAD, PAIR), jnp.float32)
    for k in range(HALF_TX):
        padded[PAD : PAD + BLOCKS] = ref[k].astype(jnp.float32)
        start = PAD - 1 - (params[first + k] + DELAYS - 1) // BLOCK_LEN
        window = jnp.concatenate(
            [padded[pl.ds(start + e, BLOCKS), :].astype(jnp.bfloat16) for e in range(4)], axis=1
        )
        out_ref[k] = nt_dot(table_ref[...], jnp.concatenate([window, window], axis=1))


def surv_spectrum(table_ref, s):
    return nt_dot(table_ref[...], jnp.concatenate([s, s], axis=1))


def surv_spectra_kernel(table_ref, s_ref, out_ref):
    for b in range(s_ref.shape[0]):
        out_ref[b] = surv_spectrum(table_ref, s_ref[b])


def surv_spectra(table, surv, name):
    return pl.pallas_call(
        surv_spectra_kernel,
        in_specs=[VMEM] * 2,
        out_specs=VMEM,
        out_shape=jax.ShapeDtypeStruct((surv.shape[0], 2 * FFT, BLOCKS), jnp.float32),
        compiler_params=pltpu.CompilerParams(vmem_limit_bytes=VMEM_LIMIT),
        name=name,
    )(table, surv)


def sum_powers(segments, first, lag_ref, dop_ref, prods, corrs, emit):
    count = segments[0][0].shape[0]
    rows = count * DELAYS
    for k in range(HALF_TX):
        corr = corrs.at[k]
        for n, (s_ref, r_ref) in enumerate(segments):
            r_re, r_im = r_ref[k, :FFT], r_ref[k, FFT:]
            prod = prods.at[n]
            for b in range(count):
                cols = slice(b * BLOCKS, (b + 1) * BLOCKS)
                s_re, s_im = s_ref[b, :FFT], s_ref[b, FFT:]
                prod[:FFT, cols] = (s_re * r_re + s_im * r_im).astype(jnp.bfloat16)
                prod[FFT:, cols] = (s_im * r_re - s_re * r_im).astype(jnp.bfloat16)
            out = dot(lag_ref[first + k], prod[...]).astype(jnp.bfloat16)
            for b in range(count):
                cols = slice(b * BLOCKS, (b + 1) * BLOCKS)
                at = n * rows + b * DELAYS
                corr[at : at + DELAYS, :BLOCKS] = out[:DELAYS, cols]
                corr[at : at + DELAYS, BLOCKS:] = out[DELAYS:, cols]
        for b in range(0, count, TOGETHER):
            power = 0.0
            for n in range(len(segments)):
                at = n * rows + b * DELAYS
                x = dot(corr[at : at + TOGETHER * DELAYS], dop_ref[first + k])
                x_re, x_im = x[:, :DOPPLER], x[:, DOPPLER:]
                power = power + (x_re * x_re + x_im * x_im) * (1.0 / (4 * BLOCKS))
            emit(k, slice(b, b + TOGETHER), power.reshape(TOGETHER, DELAYS, DOPPLER))


def emit_chunks(own_ref, send_refs):
    each = own_ref.shape[2]

    def emit(k, at, power):
        own_ref[k, at] = power[:, :each]
        for n, ref in enumerate(send_refs):
            ref[k, at] = power[:, (n + 1) * each : (n + 2) * each].astype(jnp.bfloat16)

    return emit


def own_part_kernel(params, rtab, mine, spec, lags, dops, part_ref, padded, r_here, prods, corrs):
    first = first_tx(params, 0)
    write_ref_spectra(params, first, rtab, mine, r_here, padded)

    def emit(k, at, power):
        part_ref[k, at] = power

    sum_powers([(spec, r_here)], first, lags, dops, prods, corrs, emit)


def far_part_kernel(params, rtab, far, stab, there, part_ref, lags, dops, far_spec, own_ref, *refs):
    send_refs, (padded, r_there, prods, corrs) = refs[:-4], refs[-4:]
    first = first_tx(params, 0)
    write_ref_spectra(params, first, rtab, far, r_there, padded)
    surv_spectra_kernel(stab, there, far_spec)
    store = emit_chunks(own_ref, send_refs)
    emit = lambda k, at, power: store(k, at, power + part_ref[k, at])
    sum_powers([(far_spec, r_there)], first, lags, dops, prods, corrs, emit)


def both_kernel(
    params, rtab, mine, far, spec, far_spec, near_ref, lags, dops, own_ref, near_all, *refs
):
    send_refs, (padded, r_here, r_there, prods, corrs) = refs[:-5], refs[-5:]
    first = first_tx(params, 1)
    write_ref_spectra(params, first, rtab, mine, r_here, padded)
    write_ref_spectra(params, first, rtab, far, r_there, padded)
    near_all[:HALF_TX] = near_ref[...]
    emit = emit_chunks(own_ref, (near_all.at[HALF_TX:], *send_refs))
    sum_powers([(spec, r_here), (far_spec, r_there)], first, lags, dops, prods, corrs, emit)


def assemble_kernel(n_seg, params, near_ref, *refs):
    groups, (out_ref, mean, sems) = refs[:-3], refs[-3:]
    half = out_ref.shape[1] // 2
    part = params[2 * TX + 1] % 2

    def total(values):
        return functools.reduce(jnp.add, [v.astype(jnp.float32) for v in values]) * (1.0 / n_seg)

    copies = []
    for g in range(2):
        own, *arrived = groups[g * (n_seg - 1) : (g + 1) * (n_seg - 1)]
        for k in range(HALF_TX):
            at = g * HALF_TX + k
            mean[at, pl.ds(part * half, half)] = total([r[k] for r in (own, *arrived[0::2])])
            theirs = total([near_ref[at]] + [r[k] for r in arrived[1::2]])
            mean[at, pl.ds((1 - part) * half, half)] = theirs
            copy = pltpu.make_async_copy(
                mean.at[at], out_ref.at[first_tx(params, g) + k], sems.at[at]
            )
            copy.start()
            copies.append(copy)
    for copy in copies:
        copy.wait()


def call_powers(kernel, name, args, out_shape, count, segments, flops):
    return pl.pallas_call(
        kernel,
        in_specs=[SMEM if a.ndim == 1 else VMEM for a in args],
        out_specs=[VMEM] * len(out_shape),
        out_shape=out_shape,
        scratch_shapes=[pltpu.VMEM((BLOCKS + 2 * PAD, PAIR), jnp.float32)]
        + [pltpu.VMEM((HALF_TX, 2 * FFT, BLOCKS), jnp.float32)] * segments
        + [
            pltpu.VMEM((segments, 2 * FFT, count * BLOCKS), jnp.bfloat16),
            pltpu.VMEM((HALF_TX, segments * count * DELAYS, 2 * BLOCKS), jnp.bfloat16),
        ],
        compiler_params=pltpu.CompilerParams(vmem_limit_bytes=VMEM_LIMIT * count // 8),
        cost_estimate=pl.CostEstimate(flops=flops, bytes_accessed=1 << 20, transcendentals=0),
        name=name,
    )(*args)


def swap(value, axis, flip):
    size = lax.axis_size(axis)
    return lax.ppermute(value, axis, [(i, i ^ flip) for i in range(size)])


def shards(voltages, surv_taps, ref_taps, tx_owner, delay_start, doppler_start):
    beams_here = voltages.shape[1]
    n_beam = lax.axis_size("beam")
    n_seg = lax.axis_size("seg")
    ids = jnp.stack([lax.axis_index("beam"), lax.axis_index("seg")]).astype(jnp.int32)
    volts = voltages.reshape(2, beams_here, voltages.shape[3])
    out = decimate(
        volts,
        surv_taps.reshape(1, TAPS),
        ref_taps.reshape(1, TAPS),
        ids,
        tx_owner,
        delay_start,
        doppler_start,
    )
    here, give, keep, send, params = out
    stab, rtab = jnp.asarray(surv_fourier()), jnp.asarray(ref_fourier())
    there = swap(give, "seg", 1)
    half = keep + swap(send, "beam", 1)
    half, here, params = lax.optimization_barrier((half, here, params))
    got = [swap(half, "beam", flip) for flip in range(2, n_beam, 2)]
    lags, dops = make_tables(params, n_seg)
    spec = surv_spectra(stab, here, "own_spectra")
    got, lags, dops, spec = lax.optimization_barrier((got, lags, dops, spec))
    half = functools.reduce(jnp.add, got, half)
    other = swap(half, "beam", 1)
    far = swap(half, "seg", 1)
    far_other = swap(other, "seg", 1)
    count = beams_here // 2
    each = DELAYS // n_seg
    kept = lambda n: jax.ShapeDtypeStruct((HALF_TX, count, n, DOPPLER), jnp.float32)
    sent = lambda n: jax.ShapeDtypeStruct((n, count, each, DOPPLER), jnp.bfloat16)
    (part,) = call_powers(
        own_part_kernel,
        "own_part",
        (params, rtab, half, spec, lags, dops),
        [kept(DELAYS)],
        count,
        1,
        OWN_FLOPS,
    )
    part, there = lax.optimization_barrier((part, there))
    far_spec, own, near, *long_way = call_powers(
        far_part_kernel,
        "far_part",
        (params, rtab, far, stab, there, part, lags, dops),
        [jax.ShapeDtypeStruct(spec.shape, spec.dtype), kept(each)] + [sent(HALF_TX)] * (n_seg - 1),
        count,
        1,
        FAR_FLOPS,
    )
    arrived = [swap(s, "seg", n) for n, s in enumerate(long_way, 2)]
    collected = [own] + arrived
    own, near, *long_way = call_powers(
        both_kernel,
        "both",
        (params, rtab, other, far_other, spec, far_spec, near, lags, dops),
        [kept(each), sent(TX)] + [sent(HALF_TX)] * (n_seg - 2),
        count,
        2,
        BOTH_FLOPS,
    )
    near = swap(near, "seg", 1)
    long_way[0], *arrived = lax.optimization_barrier((long_way[0], *arrived))
    collected += [own] + [swap(s, "seg", n) for n, s in enumerate(long_way, 2)]
    out = (TX, beams_here, each, DOPPLER)
    return pl.pallas_call(
        functools.partial(assemble_kernel, n_seg),
        in_specs=[SMEM] + [VMEM] * (1 + len(collected)),
        out_specs=pl.BlockSpec(memory_space=pl.ANY),
        out_shape=jax.ShapeDtypeStruct(out, jnp.float32),
        scratch_shapes=[pltpu.VMEM(out, jnp.float32), pltpu.SemaphoreType.DMA((TX,))],
        compiler_params=pltpu.CompilerParams(vmem_limit_bytes=VMEM_LIMIT),
        name="assemble",
    )(params, near, *collected)


def solution(mesh):
    return jax.shard_map(
        shards,
        mesh=mesh,
        in_specs=(P(None, "beam", "seg", None), P(), P(), P(), P(), P()),
        out_specs=P(None, "beam", "seg", None),
        check_vma=False,
    )
```

```python
import functools

import jax
import jax.numpy as jnp
import ml_dtypes
import numpy as np
from jax import lax
from jax.experimental import pallas as pl
from jax.experimental.pallas import tpu as pltpu
from jax.sharding import PartitionSpec as P

TX = 4
HALF_TX = TX // 2
DECIM = 4
TAPS = 32
BLOCK_LEN = 64
BLOCKS = 256
DELAYS = 128
DOPPLER = 128
FFT = 256
STRIDE = DECIM * BLOCK_LEN
LEAD = 128
REACH = LEAD + STRIDE
PAIR = 2 * BLOCK_LEN
TOGETHER = 4
LANES = 128
LANE_BLOCKS = 2 * FFT // LANES
VMEM_LIMIT = 24 * 1024 * 1024
OWN_FLOPS = 1_600_000_000
FAR_FLOPS = 1_600_000_000
BOTH_FLOPS = 3_200_000_000

SMEM = pl.BlockSpec(memory_space=pltpu.SMEM)
VMEM = pl.BlockSpec(memory_space=pltpu.VMEM)
HBM = pl.BlockSpec(memory_space=pltpu.HBM)


def split_bf16(table):
    hi = table.astype(ml_dtypes.bfloat16)
    lo = (table - hi.astype(np.float64)).astype(ml_dtypes.bfloat16)
    return hi, lo


def fourier(samples):
    angle = 2 * np.pi / FFT * (np.outer(np.arange(FFT), samples) % FFT)
    cos, sin = np.cos(angle), np.sin(angle)
    return np.block([[cos, sin], [-sin, cos]])


def surv_fourier():
    hi, lo = split_bf16(fourier(np.arange(BLOCK_LEN)))
    return np.concatenate([hi, lo], axis=1)


def ref_fourier():
    parts = [fourier(np.arange(BLOCK_LEN) + BLOCK_LEN * e) for e in range(4)]
    hi, lo = split_bf16(np.concatenate(parts, axis=1))
    return np.concatenate([hi, lo], axis=1)


def in_lane_blocks(both):
    parts, rows, _ = both.shape
    return both.astype(np.float32).reshape(parts, rows, LANE_BLOCKS, LANES).swapaxes(1, 2)


def lag_table():
    lags = 191 - np.arange(192)
    angle = 2 * np.pi / FFT * (np.outer(lags, np.arange(FFT)) % FFT)
    cos, sin = np.cos(angle), np.sin(angle)
    scale = 1.0 / (FFT * np.sqrt(BLOCK_LEN))
    both = np.stack([np.concatenate([cos, sin], 1), np.concatenate([-sin, cos], 1)])
    both = both.astype(ml_dtypes.bfloat16).astype(np.float64) * scale
    return in_lane_blocks(both)


def doppler_table():
    freqs = np.arange(BLOCKS) - BLOCKS // 2
    angle = 2 * np.pi / BLOCKS * (np.outer(freqs, np.arange(BLOCKS)) % BLOCKS)
    cos, sin = np.cos(angle), np.sin(angle)
    both = np.stack([np.concatenate([cos, sin], 1), np.concatenate([-sin, cos], 1)])
    return in_lane_blocks(both.astype(ml_dtypes.bfloat16))


def nt_dot(left, right):
    return lax.dot_general(
        left, right, (((1,), (1,)), ((), ())), preferred_element_type=jnp.float32
    )


def dot(left, right):
    return jnp.dot(left, right, preferred_element_type=jnp.float32)


def decimate_kernel(beams, ids, owner, delay, doppler, staps, rtaps, volts, *refs):
    here_ref, give_ref, keep_ref, send_ref, params, x, taps, small, band, all_s, all_r, sems, small_sems = refs
    chunks = sems.shape[0]
    raw = volts.shape[2]
    wide = raw // chunks
    rows = wide // STRIDE
    blocks = raw // STRIDE
    smalls = [
        pltpu.make_async_copy(ref, small.at[n], small_sems.at[n])
        for n, ref in enumerate((owner, delay, doppler))
    ]
    smalls += [
        pltpu.make_async_copy(ref, taps.at[n], small_sems.at[3 + n])
        for n, ref in enumerate((staps, rtaps))
    ]
    copies = [
        pltpu.make_async_copy(
            volts.at[:, :, pl.ds(n * wide, wide)],
            x.at[:, :, pl.ds(LEAD + n * wide, wide)],
            sems.at[n],
        )
        for n in range(chunks)
    ]
    for copy in smalls + copies:
        copy.start()
    x[:, :, :LEAD] = jnp.zeros((2, beams, LEAD), jnp.bfloat16)
    for copy in smalls:
        copy.wait()

    shape = (REACH, PAIR)
    q = lax.broadcasted_iota(jnp.int32, shape, 0)
    lane = lax.broadcasted_iota(jnp.int32, shape, 1)
    tap = LEAD + DECIM * (lane % BLOCK_LEN) - q
    first = lane < BLOCK_LEN
    one, two = taps[0].astype(jnp.float32), taps[1].astype(jnp.float32)
    both = jnp.zeros(shape, jnp.float32)
    for t in range(TAPS):
        row = jnp.where(first[:1], one[:, t : t + 1], two[:, t : t + 1])
        both = jnp.where(tap == t, row, both)
    turned = pltpu.roll(both, BLOCK_LEN, 1)
    zero = jnp.zeros(shape, jnp.float32)
    band[:REACH, :PAIR] = jnp.where(first, both, zero).astype(jnp.bfloat16)
    band[REACH:, :PAIR] = jnp.where(first, zero, turned).astype(jnp.bfloat16)
    band[:REACH, PAIR:] = jnp.where(first, turned, zero).astype(jnp.bfloat16)
    band[REACH:, PAIR:] = jnp.where(first, zero, both).astype(jnp.bfloat16)
    for k in range(TX):
        params[k] = small[1, k]
        params[TX + k] = small[2, k]
    params[2 * TX] = ids[0]
    params[2 * TX + 1] = ids[1]

    def step(n, _):
        pltpu.make_async_copy(
            volts.at[:, :, pl.ds(n * wide, wide)],
            x.at[:, :, pl.ds(LEAD + n * wide, wide)],
            sems.at[n],
        ).wait()
        parts = []
        for c in range(2):
            starts = [pl.multiple_of(n * wide + l * STRIDE, STRIDE) for l in range(rows)]
            parts.append(jnp.concatenate([x[c, :, pl.ds(at, REACH)] for at in starts], axis=0))
        out = dot(jnp.concatenate(parts, axis=1), band[...])
        span = pl.ds(pl.multiple_of(n * rows * beams, rows * beams), rows * beams)
        all_s[span] = out[:, :PAIR]
        all_r[span] = out[:, PAIR:]
        here = pl.ds(pl.multiple_of(n * rows, rows), rows)
        part = ids[1] % 2
        half = beams // 2
        for s_ref, at in ((here_ref, part * half), (give_ref, (1 - part) * half)):
            for b in range(half):
                picked = all_s[pl.ds(n * rows * beams + at + b, rows, stride=beams), :]
                s_ref[b, here] = picked.astype(jnp.bfloat16)
        return 0

    lax.fori_loop(0, chunks, step, 0)
    core = ids[0] % 2
    for ref, first_tx in ((keep_ref, core * HALF_TX), (send_ref, (1 - core) * HALF_TX)):
        for k in range(HALF_TX):
            beam = small[0, first_tx + k]
            picked = all_r[pl.ds(beam % beams, blocks, stride=beams), :]
            ref[k] = jnp.where(beam // beams == ids[0], picked, 0.0).astype(jnp.bfloat16)


def decimate(volts, staps, rtaps, ids, owner, delay, doppler):
    beams, raw = volts.shape[1:]
    blocks = raw // STRIDE
    chunks = 1
    arrays = (owner, delay, doppler, staps, rtaps, volts)
    shape = lambda n: jax.ShapeDtypeStruct((n, blocks, PAIR), jnp.bfloat16)
    return pl.pallas_call(
        functools.partial(decimate_kernel, beams),
        in_specs=[SMEM] + [HBM] * 6,
        out_specs=[VMEM] * 4 + [SMEM],
        out_shape=[shape(beams // 2)] * 2
        + [shape(HALF_TX)] * 2
        + [jax.ShapeDtypeStruct((2 * TX + 2,), jnp.int32)],
        scratch_shapes=[
            pltpu.VMEM((2, beams, LEAD + raw), jnp.bfloat16),
            pltpu.VMEM((2, 1, TAPS), jnp.bfloat16),
            pltpu.SMEM((3, TX), jnp.int32),
            pltpu.VMEM((2 * REACH, 2 * PAIR), jnp.bfloat16),
            pltpu.VMEM((blocks * beams + beams, PAIR), jnp.float32),
            pltpu.VMEM((blocks * beams + beams, PAIR), jnp.float32),
            pltpu.SemaphoreType.DMA((chunks,)),
            pltpu.SemaphoreType.DMA((5,)),
        ],
        compiler_params=pltpu.CompilerParams(vmem_limit_bytes=VMEM_LIMIT),
        name="decimate",
    )(ids, *(pltpu.with_memory_space_constraint(a, pltpu.HBM) for a in arrays))


def tables_kernel(chunks, params, lag_ref, dop_ref, lags, dops):
    each = DELAYS // chunks
    for k in range(TX):
        base = (params[k] + DELAYS - 1) % BLOCK_LEN
        for part in range(2):
            for n in range(chunks):
                chunk = params[2 * TX + 1] ^ n
                at = part * DELAYS + n * each
                for q in range(LANE_BLOCKS):
                    picked = lag_ref[part, q, pl.ds(base + chunk * each, each), :]
                    lags[k, at : at + each, q * LANES : (q + 1) * LANES] = picked.astype(jnp.bfloat16)
            for q in range(LANE_BLOCKS):
                picked = dop_ref[part, q, pl.ds(params[TX + k], DOPPLER), :].T.astype(jnp.bfloat16)
                dops[k, q * LANES : (q + 1) * LANES, part * DOPPLER : (part + 1) * DOPPLER] = picked


def make_tables(params, chunks):
    return pl.pallas_call(
        functools.partial(tables_kernel, chunks),
        in_specs=[SMEM, VMEM, VMEM],
        out_specs=[VMEM, VMEM],
        out_shape=[
            jax.ShapeDtypeStruct((TX, 2 * DELAYS, 2 * FFT), jnp.bfloat16),
            jax.ShapeDtypeStruct((TX, 2 * BLOCKS, 2 * DOPPLER), jnp.bfloat16),
        ],
        compiler_params=pltpu.CompilerParams(vmem_limit_bytes=VMEM_LIMIT),
        name="tables",
    )(params, jnp.asarray(lag_table()), jnp.asarray(doppler_table()))


PAD = 8


def first_tx(params, group):
    core = params[2 * TX] % 2
    return (core if group == 0 else 1 - core) * HALF_TX


def write_ref_spectra(params, first, table_ref, ref, out_ref, padded):
    padded[:PAD] = jnp.zeros((PAD, PAIR), jnp.float32)
    padded[PAD + BLOCKS :] = jnp.zeros((PAD, PAIR), jnp.float32)
    for k in range(HALF_TX):
        padded[PAD : PAD + BLOCKS] = ref[k].astype(jnp.float32)
        start = PAD - 1 - (params[first + k] + DELAYS - 1) // BLOCK_LEN
        window = jnp.concatenate(
            [padded[pl.ds(start + e, BLOCKS), :].astype(jnp.bfloat16) for e in range(4)], axis=1
        )
        out_ref[k] = nt_dot(table_ref[...], jnp.concatenate([window, window], axis=1))


def surv_spectrum(table_ref, s):
    return nt_dot(table_ref[...], jnp.concatenate([s, s], axis=1))


def surv_spectra_kernel(table_ref, s_ref, out_ref):
    for b in range(s_ref.shape[0]):
        out_ref[b] = surv_spectrum(table_ref, s_ref[b])


def surv_spectra(table, surv, name):
    return pl.pallas_call(
        surv_spectra_kernel,
        in_specs=[VMEM] * 2,
        out_specs=VMEM,
        out_shape=jax.ShapeDtypeStruct((surv.shape[0], 2 * FFT, BLOCKS), jnp.float32),
        compiler_params=pltpu.CompilerParams(vmem_limit_bytes=VMEM_LIMIT),
        name=name,
    )(table, surv)


def sum_powers(segments, first, lag_ref, dop_ref, prods, corrs, emit):
    count = segments[0][0].shape[0]
    rows = count * DELAYS
    for k in range(HALF_TX):
        corr = corrs.at[k]
        for n, (s_ref, r_ref) in enumerate(segments):
            r_re, r_im = r_ref[k, :FFT], r_ref[k, FFT:]
            prod = prods.at[n]
            for b in range(count):
                cols = slice(b * BLOCKS, (b + 1) * BLOCKS)
                s_re, s_im = s_ref[b, :FFT], s_ref[b, FFT:]
                prod[:FFT, cols] = (s_re * r_re + s_im * r_im).astype(jnp.bfloat16)
                prod[FFT:, cols] = (s_im * r_re - s_re * r_im).astype(jnp.bfloat16)
            out = dot(lag_ref[first + k], prod[...]).astype(jnp.bfloat16)
            for b in range(count):
                cols = slice(b * BLOCKS, (b + 1) * BLOCKS)
                at = n * rows + b * DELAYS
                corr[at : at + DELAYS, :BLOCKS] = out[:DELAYS, cols]
                corr[at : at + DELAYS, BLOCKS:] = out[DELAYS:, cols]
        for b in range(0, count, TOGETHER):
            power = 0.0
            for n in range(len(segments)):
                at = n * rows + b * DELAYS
                x = dot(corr[at : at + TOGETHER * DELAYS], dop_ref[first + k])
                x_re, x_im = x[:, :DOPPLER], x[:, DOPPLER:]
                power = power + (x_re * x_re + x_im * x_im) * (1.0 / (4 * BLOCKS))
            emit(k, slice(b, b + TOGETHER), power.reshape(TOGETHER, DELAYS, DOPPLER))


def emit_chunks(own_ref, send_refs):
    each = own_ref.shape[2]

    def emit(k, at, power):
        own_ref[k, at] = power[:, :each]
        for n, ref in enumerate(send_refs):
            ref[k, at] = power[:, (n + 1) * each : (n + 2) * each].astype(jnp.bfloat16)

    return emit


def own_part_kernel(params, rtab, mine, spec, lags, dops, part_ref, padded, r_here, prods, corrs):
    first = first_tx(params, 0)
    write_ref_spectra(params, first, rtab, mine, r_here, padded)

    def emit(k, at, power):
        part_ref[k, at] = power

    sum_powers([(spec, r_here)], first, lags, dops, prods, corrs, emit)


def far_part_kernel(params, rtab, far, stab, there, part_ref, lags, dops, far_spec, own_ref, *refs):
    send_refs, (padded, r_there, prods, corrs) = refs[:-4], refs[-4:]
    first = first_tx(params, 0)
    write_ref_spectra(params, first, rtab, far, r_there, padded)
    surv_spectra_kernel(stab, there, far_spec)
    store = emit_chunks(own_ref, send_refs)
    emit = lambda k, at, power: store(k, at, power + part_ref[k, at])
    sum_powers([(far_spec, r_there)], first, lags, dops, prods, corrs, emit)


def both_kernel(
    params, rtab, mine, far, spec, far_spec, near_ref, lags, dops, own_ref, near_all, *refs
):
    send_refs, (padded, r_here, r_there, prods, corrs) = refs[:-5], refs[-5:]
    first = first_tx(params, 1)
    write_ref_spectra(params, first, rtab, mine, r_here, padded)
    write_ref_spectra(params, first, rtab, far, r_there, padded)
    near_all[:HALF_TX] = near_ref[...]
    emit = emit_chunks(own_ref, (near_all.at[HALF_TX:], *send_refs))
    sum_powers([(spec, r_here), (far_spec, r_there)], first, lags, dops, prods, corrs, emit)


def assemble_kernel(n_seg, params, near_ref, *refs):
    groups, (out_ref, mean, sems) = refs[:-3], refs[-3:]
    half = out_ref.shape[1] // 2
    part = params[2 * TX + 1] % 2

    def total(values):
        return functools.reduce(jnp.add, [v.astype(jnp.float32) for v in values]) * (1.0 / n_seg)

    copies = []
    for g in range(2):
        own, *arrived = groups[g * (n_seg - 1) : (g + 1) * (n_seg - 1)]
        for k in range(HALF_TX):
            at = g * HALF_TX + k
            mean[at, pl.ds(part * half, half)] = total([r[k] for r in (own, *arrived[0::2])])
            theirs = total([near_ref[at]] + [r[k] for r in arrived[1::2]])
            mean[at, pl.ds((1 - part) * half, half)] = theirs
            copy = pltpu.make_async_copy(
                mean.at[at], out_ref.at[first_tx(params, g) + k], sems.at[at]
            )
            copy.start()
            copies.append(copy)
    for copy in copies:
        copy.wait()


def call_powers(kernel, name, args, out_shape, count, segments, flops):
    return pl.pallas_call(
        kernel,
        in_specs=[SMEM if a.ndim == 1 else VMEM for a in args],
        out_specs=[VMEM] * len(out_shape),
        out_shape=out_shape,
        scratch_shapes=[pltpu.VMEM((BLOCKS + 2 * PAD, PAIR), jnp.float32)]
        + [pltpu.VMEM((HALF_TX, 2 * FFT, BLOCKS), jnp.float32)] * segments
        + [
            pltpu.VMEM((segments, 2 * FFT, count * BLOCKS), jnp.bfloat16),
            pltpu.VMEM((HALF_TX, segments * count * DELAYS, 2 * BLOCKS), jnp.bfloat16),
        ],
        compiler_params=pltpu.CompilerParams(vmem_limit_bytes=VMEM_LIMIT * count // 8),
        cost_estimate=pl.CostEstimate(flops=flops, bytes_accessed=1 << 20, transcendentals=0),
        name=name,
    )(*args)


def swap(value, axis, flip):
    size = lax.axis_size(axis)
    return lax.ppermute(value, axis, [(i, i ^ flip) for i in range(size)])


def shards(voltages, surv_taps, ref_taps, tx_owner, delay_start, doppler_start):
    beams_here = voltages.shape[1]
    n_beam = lax.axis_size("beam")
    n_seg = lax.axis_size("seg")
    ids = jnp.stack([lax.axis_index("beam"), lax.axis_index("seg")]).astype(jnp.int32)
    volts = voltages.reshape(2, beams_here, voltages.shape[3])
    out = decimate(
        volts,
        surv_taps.reshape(1, TAPS),
        ref_taps.reshape(1, TAPS),
        ids,
        tx_owner,
        delay_start,
        doppler_start,
    )
    here, give, keep, send, params = out
    stab, rtab = jnp.asarray(surv_fourier()), jnp.asarray(ref_fourier())
    there = swap(give, "seg", 1)
    half = keep + swap(send, "beam", 1)
    half, here, params = lax.optimization_barrier((half, here, params))
    got = [swap(half, "beam", flip) for flip in range(2, n_beam, 2)]
    lags, dops = make_tables(params, n_seg)
    spec = surv_spectra(stab, here, "own_spectra")
    got, lags, dops, spec = lax.optimization_barrier((got, lags, dops, spec))
    half = functools.reduce(jnp.add, got, half)
    other = swap(half, "beam", 1)
    far = swap(half, "seg", 1)
    far_other = swap(other, "seg", 1)
    count = beams_here // 2
    each = DELAYS // n_seg
    kept = lambda n: jax.ShapeDtypeStruct((HALF_TX, count, n, DOPPLER), jnp.float32)
    sent = lambda n: jax.ShapeDtypeStruct((n, count, each, DOPPLER), jnp.bfloat16)
    (part,) = call_powers(
        own_part_kernel,
        "own_part",
        (params, rtab, half, spec, lags, dops),
        [kept(DELAYS)],
        count,
        1,
        OWN_FLOPS,
    )
    part, there = lax.optimization_barrier((part, there))
    far_spec, own, near, *long_way = call_powers(
        far_part_kernel,
        "far_part",
        (params, rtab, far, stab, there, part, lags, dops),
        [jax.ShapeDtypeStruct(spec.shape, spec.dtype), kept(each)] + [sent(HALF_TX)] * (n_seg - 1),
        count,
        1,
        FAR_FLOPS,
    )
    arrived = [swap(s, "seg", n) for n, s in enumerate(long_way, 2)]
    collected = [own] + arrived
    own, near, *long_way = call_powers(
        both_kernel,
        "both",
        (params, rtab, other, far_other, spec, far_spec, near, lags, dops),
        [kept(each), sent(TX)] + [sent(HALF_TX)] * (n_seg - 2),
        count,
        2,
        BOTH_FLOPS,
    )
    near = swap(near, "seg", 1)
    long_way[0], *arrived = lax.optimization_barrier((long_way[0], *arrived))
    collected += [own] + [swap(s, "seg", n) for n, s in enumerate(long_way, 2)]
    out = (TX, beams_here, each, DOPPLER)
    return pl.pallas_call(
        functools.partial(assemble_kernel, n_seg),
        in_specs=[SMEM] + [VMEM] * (1 + len(collected)),
        out_specs=pl.BlockSpec(memory_space=pl.ANY),
        out_shape=jax.ShapeDtypeStruct(out, jnp.float32),
        scratch_shapes=[pltpu.VMEM(out, jnp.float32), pltpu.SemaphoreType.DMA((TX,))],
        compiler_params=pltpu.CompilerParams(vmem_limit_bytes=VMEM_LIMIT),
        name="assemble",
    )(params, near, *collected)


def solution(mesh):
    return jax.shard_map(
        shards,
        mesh=mesh,
        in_specs=(P(None, "beam", "seg", None), P(), P(), P(), P(), P()),
        out_specs=P(None, "beam", "seg", None),
        check_vma=False,
    )
```

```python
import functools

import jax
import jax.numpy as jnp
import ml_dtypes
import numpy as np
from jax import lax
from jax.experimental import pallas as pl
from jax.experimental.pallas import tpu as pltpu
from jax.sharding import PartitionSpec as P

TX = 4
HALF_TX = TX // 2
DECIM = 4
TAPS = 32
BLOCK_LEN = 64
BLOCKS = 256
DELAYS = 128
DOPPLER = 128
FFT = 256
STRIDE = DECIM * BLOCK_LEN
LEAD = 128
REACH = LEAD + STRIDE
PAIR = 2 * BLOCK_LEN
TOGETHER = 4
LANES = 128
LANE_BLOCKS = 2 * FFT // LANES
VMEM_LIMIT = 24 * 1024 * 1024
OWN_FLOPS = 1_600_000_000
FAR_FLOPS = 1_600_000_000
BOTH_FLOPS = 3_200_000_000

SMEM = pl.BlockSpec(memory_space=pltpu.SMEM)
VMEM = pl.BlockSpec(memory_space=pltpu.VMEM)
HBM = pl.BlockSpec(memory_space=pltpu.HBM)


def split_bf16(table):
    hi = table.astype(ml_dtypes.bfloat16)
    lo = (table - hi.astype(np.float64)).astype(ml_dtypes.bfloat16)
    return hi, lo


def fourier(samples):
    angle = 2 * np.pi / FFT * (np.outer(np.arange(FFT), samples) % FFT)
    cos, sin = np.cos(angle), np.sin(angle)
    return np.block([[cos, sin], [-sin, cos]])


def surv_fourier():
    hi, lo = split_bf16(fourier(np.arange(BLOCK_LEN)))
    return np.concatenate([hi, lo], axis=1)


def ref_fourier():
    parts = [fourier(np.arange(BLOCK_LEN) + BLOCK_LEN * e) for e in range(4)]
    hi, lo = split_bf16(np.concatenate(parts, axis=1))
    return np.concatenate([hi, lo], axis=1)


def in_lane_blocks(both):
    parts, rows, _ = both.shape
    return both.astype(np.float32).reshape(parts, rows, LANE_BLOCKS, LANES).swapaxes(1, 2)


def lag_table():
    lags = 191 - np.arange(192)
    angle = 2 * np.pi / FFT * (np.outer(lags, np.arange(FFT)) % FFT)
    cos, sin = np.cos(angle), np.sin(angle)
    scale = 1.0 / (FFT * np.sqrt(BLOCK_LEN))
    both = np.stack([np.concatenate([cos, sin], 1), np.concatenate([-sin, cos], 1)])
    both = both.astype(ml_dtypes.bfloat16).astype(np.float64) * scale
    return in_lane_blocks(both)


def doppler_table():
    freqs = np.arange(BLOCKS) - BLOCKS // 2
    angle = 2 * np.pi / BLOCKS * (np.outer(freqs, np.arange(BLOCKS)) % BLOCKS)
    cos, sin = np.cos(angle), np.sin(angle)
    both = np.stack([np.concatenate([cos, sin], 1), np.concatenate([-sin, cos], 1)])
    return in_lane_blocks(both.astype(ml_dtypes.bfloat16))


def nt_dot(left, right):
    return lax.dot_general(
        left, right, (((1,), (1,)), ((), ())), preferred_element_type=jnp.float32
    )


def dot(left, right):
    return jnp.dot(left, right, preferred_element_type=jnp.float32)


def decimate_kernel(beams, ids, owner, delay, doppler, staps, rtaps, volts, *refs):
    here_ref, give_ref, keep_ref, send_ref, params, x, taps, small, band, all_s, all_r, sems, small_sems = refs
    chunks = sems.shape[0]
    raw = volts.shape[2]
    wide = raw // chunks
    rows = wide // STRIDE
    blocks = raw // STRIDE
    smalls = [
        pltpu.make_async_copy(ref, small.at[n], small_sems.at[n])
        for n, ref in enumerate((owner, delay, doppler))
    ]
    smalls += [
        pltpu.make_async_copy(ref, taps.at[n], small_sems.at[3 + n])
        for n, ref in enumerate((staps, rtaps))
    ]
    copies = [
        pltpu.make_async_copy(
            volts.at[:, :, pl.ds(n * wide, wide)],
            x.at[:, :, pl.ds(LEAD + n * wide, wide)],
            sems.at[n],
        )
        for n in range(chunks)
    ]
    for copy in smalls + copies:
        copy.start()
    x[:, :, :LEAD] = jnp.zeros((2, beams, LEAD), jnp.bfloat16)
    for copy in smalls:
        copy.wait()

    shape = (REACH, PAIR)
    q = lax.broadcasted_iota(jnp.int32, shape, 0)
    lane = lax.broadcasted_iota(jnp.int32, shape, 1)
    tap = LEAD + DECIM * (lane % BLOCK_LEN) - q
    first = lane < BLOCK_LEN
    one, two = taps[0].astype(jnp.float32), taps[1].astype(jnp.float32)
    both = jnp.zeros(shape, jnp.float32)
    for t in range(TAPS):
        row = jnp.where(first[:1], one[:, t : t + 1], two[:, t : t + 1])
        both = jnp.where(tap == t, row, both)
    turned = pltpu.roll(both, BLOCK_LEN, 1)
    zero = jnp.zeros(shape, jnp.float32)
    band[:REACH, :PAIR] = jnp.where(first, both, zero).astype(jnp.bfloat16)
    band[REACH:, :PAIR] = jnp.where(first, zero, turned).astype(jnp.bfloat16)
    band[:REACH, PAIR:] = jnp.where(first, turned, zero).astype(jnp.bfloat16)
    band[REACH:, PAIR:] = jnp.where(first, zero, both).astype(jnp.bfloat16)
    for k in range(TX):
        params[k] = small[1, k]
        params[TX + k] = small[2, k]
    params[2 * TX] = ids[0]
    params[2 * TX + 1] = ids[1]

    def step(n, _):
        pltpu.make_async_copy(
            volts.at[:, :, pl.ds(n * wide, wide)],
            x.at[:, :, pl.ds(LEAD + n * wide, wide)],
            sems.at[n],
        ).wait()
        parts = []
        for c in range(2):
            starts = [pl.multiple_of(n * wide + l * STRIDE, STRIDE) for l in range(rows)]
            parts.append(jnp.concatenate([x[c, :, pl.ds(at, REACH)] for at in starts], axis=0))
        out = dot(jnp.concatenate(parts, axis=1), band[...])
        span = pl.ds(pl.multiple_of(n * rows * beams, rows * beams), rows * beams)
        all_s[span] = out[:, :PAIR]
        all_r[span] = out[:, PAIR:]
        here = pl.ds(pl.multiple_of(n * rows, rows), rows)
        part = ids[1] % 2
        half = beams // 2
        for s_ref, at in ((here_ref, part * half), (give_ref, (1 - part) * half)):
            for b in range(half):
                picked = all_s[pl.ds(n * rows * beams + at + b, rows, stride=beams), :]
                s_ref[b, here] = picked.astype(jnp.bfloat16)
        return 0

    lax.fori_loop(0, chunks, step, 0)
    core = ids[0] % 2
    for ref, first_tx in ((keep_ref, core * HALF_TX), (send_ref, (1 - core) * HALF_TX)):
        for k in range(HALF_TX):
            beam = small[0, first_tx + k]
            picked = all_r[pl.ds(beam % beams, blocks, stride=beams), :]
            ref[k] = jnp.where(beam // beams == ids[0], picked, 0.0).astype(jnp.bfloat16)


def decimate(volts, staps, rtaps, ids, owner, delay, doppler):
    beams, raw = volts.shape[1:]
    blocks = raw // STRIDE
    chunks = 1
    arrays = (owner, delay, doppler, staps, rtaps, volts)
    shape = lambda n: jax.ShapeDtypeStruct((n, blocks, PAIR), jnp.bfloat16)
    return pl.pallas_call(
        functools.partial(decimate_kernel, beams),
        in_specs=[SMEM] + [HBM] * 6,
        out_specs=[VMEM] * 4 + [SMEM],
        out_shape=[shape(beams // 2)] * 2
        + [shape(HALF_TX)] * 2
        + [jax.ShapeDtypeStruct((2 * TX + 2,), jnp.int32)],
        scratch_shapes=[
            pltpu.VMEM((2, beams, LEAD + raw), jnp.bfloat16),
            pltpu.VMEM((2, 1, TAPS), jnp.bfloat16),
            pltpu.SMEM((3, TX), jnp.int32),
            pltpu.VMEM((2 * REACH, 2 * PAIR), jnp.bfloat16),
            pltpu.VMEM((blocks * beams + beams, PAIR), jnp.float32),
            pltpu.VMEM((blocks * beams + beams, PAIR), jnp.float32),
            pltpu.SemaphoreType.DMA((chunks,)),
            pltpu.SemaphoreType.DMA((5,)),
        ],
        compiler_params=pltpu.CompilerParams(vmem_limit_bytes=VMEM_LIMIT),
        name="decimate",
    )(ids, *(pltpu.with_memory_space_constraint(a, pltpu.HBM) for a in arrays))


def tables_kernel(chunks, params, lag_ref, dop_ref, lags, dops):
    each = DELAYS // chunks
    for k in range(TX):
        base = (params[k] + DELAYS - 1) % BLOCK_LEN
        for part in range(2):
            for n in range(chunks):
                chunk = params[2 * TX + 1] ^ n
                at = part * DELAYS + n * each
                for q in range(LANE_BLOCKS):
                    picked = lag_ref[part, q, pl.ds(base + chunk * each, each), :]
                    lags[k, at : at + each, q * LANES : (q + 1) * LANES] = picked.astype(jnp.bfloat16)
            for q in range(LANE_BLOCKS):
                picked = dop_ref[part, q, pl.ds(params[TX + k], DOPPLER), :].T.astype(jnp.bfloat16)
                dops[k, q * LANES : (q + 1) * LANES, part * DOPPLER : (part + 1) * DOPPLER] = picked


def make_tables(params, chunks):
    return pl.pallas_call(
        functools.partial(tables_kernel, chunks),
        in_specs=[SMEM, VMEM, VMEM],
        out_specs=[VMEM, VMEM],
        out_shape=[
            jax.ShapeDtypeStruct((TX, 2 * DELAYS, 2 * FFT), jnp.bfloat16),
            jax.ShapeDtypeStruct((TX, 2 * BLOCKS, 2 * DOPPLER), jnp.bfloat16),
        ],
        compiler_params=pltpu.CompilerParams(vmem_limit_bytes=VMEM_LIMIT),
        name="tables",
    )(params, jnp.asarray(lag_table()), jnp.asarray(doppler_table()))


PAD = 8


def first_tx(params, group):
    core = params[2 * TX] % 2
    return (core if group == 0 else 1 - core) * HALF_TX


def ref_spectra_writer(params, first, table_ref, ref, out_ref, padded):
    padded[:PAD] = jnp.zeros((PAD, PAIR), jnp.float32)
    padded[PAD + BLOCKS :] = jnp.zeros((PAD, PAIR), jnp.float32)

    def write(k):
        padded[PAD : PAD + BLOCKS] = ref[k].astype(jnp.float32)
        start = PAD - 1 - (params[first + k] + DELAYS - 1) // BLOCK_LEN
        window = jnp.concatenate(
            [padded[pl.ds(start + e, BLOCKS), :].astype(jnp.bfloat16) for e in range(4)], axis=1
        )
        out_ref[k] = nt_dot(table_ref[...], jnp.concatenate([window, window], axis=1))

    return write


def surv_spectrum(table_ref, s):
    return nt_dot(table_ref[...], jnp.concatenate([s, s], axis=1))


def surv_spectra_kernel(table_ref, s_ref, out_ref):
    for b in range(s_ref.shape[0]):
        out_ref[b] = surv_spectrum(table_ref, s_ref[b])


def surv_spectra(table, surv, name):
    return pl.pallas_call(
        surv_spectra_kernel,
        in_specs=[VMEM] * 2,
        out_specs=VMEM,
        out_shape=jax.ShapeDtypeStruct((surv.shape[0], 2 * FFT, BLOCKS), jnp.float32),
        compiler_params=pltpu.CompilerParams(vmem_limit_bytes=VMEM_LIMIT),
        name=name,
    )(table, surv)


def sum_powers(writers, segments, first, lag_ref, dop_ref, prods, corrs, emit):
    count = segments[0][0].shape[0]
    rows = count * DELAYS
    for k in range(HALF_TX):
        for write in writers:
            write(k)
        corr = corrs.at[k]
        for n, (s_ref, r_ref) in enumerate(segments):
            r_re, r_im = r_ref[k, :FFT], r_ref[k, FFT:]
            prod = prods.at[n]
            for b in range(count):
                cols = slice(b * BLOCKS, (b + 1) * BLOCKS)
                s_re, s_im = s_ref[b, :FFT], s_ref[b, FFT:]
                prod[:FFT, cols] = (s_re * r_re + s_im * r_im).astype(jnp.bfloat16)
                prod[FFT:, cols] = (s_im * r_re - s_re * r_im).astype(jnp.bfloat16)
            out = dot(lag_ref[first + k], prod[...]).astype(jnp.bfloat16)
            for b in range(count):
                cols = slice(b * BLOCKS, (b + 1) * BLOCKS)
                at = n * rows + b * DELAYS
                corr[at : at + DELAYS, :BLOCKS] = out[:DELAYS, cols]
                corr[at : at + DELAYS, BLOCKS:] = out[DELAYS:, cols]
        for b in range(0, count, TOGETHER):
            power = 0.0
            for n in range(len(segments)):
                at = n * rows + b * DELAYS
                x = dot(corr[at : at + TOGETHER * DELAYS], dop_ref[first + k])
                x_re, x_im = x[:, :DOPPLER], x[:, DOPPLER:]
                power = power + (x_re * x_re + x_im * x_im) * (1.0 / (4 * BLOCKS))
            emit(k, slice(b, b + TOGETHER), power.reshape(TOGETHER, DELAYS, DOPPLER))


def emit_chunks(own_ref, send_refs):
    each = own_ref.shape[2]

    def emit(k, at, power):
        own_ref[k, at] = power[:, :each]
        for n, ref in enumerate(send_refs):
            ref[k, at] = power[:, (n + 1) * each : (n + 2) * each].astype(jnp.bfloat16)

    return emit


def own_part_kernel(params, rtab, mine, spec, lags, dops, part_ref, padded, r_here, prods, corrs):
    first = first_tx(params, 0)
    write = ref_spectra_writer(params, first, rtab, mine, r_here, padded)
    for k in range(HALF_TX):
        write(k)

    def emit(k, at, power):
        part_ref[k, at] = power

    sum_powers([], [(spec, r_here)], first, lags, dops, prods, corrs, emit)


def far_part_kernel(params, rtab, far, stab, there, part_ref, lags, dops, far_spec, own_ref, *refs):
    send_refs, (padded, r_there, prods, corrs) = refs[:-4], refs[-4:]
    first = first_tx(params, 0)
    write = ref_spectra_writer(params, first, rtab, far, r_there, padded)
    for k in range(HALF_TX):
        write(k)
    surv_spectra_kernel(stab, there, far_spec)
    store = emit_chunks(own_ref, send_refs)
    emit = lambda k, at, power: store(k, at, power + part_ref[k, at])
    sum_powers([], [(far_spec, r_there)], first, lags, dops, prods, corrs, emit)


def both_kernel(
    params, rtab, mine, far, spec, far_spec, near_ref, lags, dops, own_ref, near_all, *refs
):
    send_refs, (padded, r_here, r_there, prods, corrs) = refs[:-5], refs[-5:]
    first = first_tx(params, 1)
    writers = [
        ref_spectra_writer(params, first, rtab, ref, out, padded)
        for ref, out in ((mine, r_here), (far, r_there))
    ]
    near_all[:HALF_TX] = near_ref[...]
    emit = emit_chunks(own_ref, (near_all.at[HALF_TX:], *send_refs))
    sum_powers(writers, [(spec, r_here), (far_spec, r_there)], first, lags, dops, prods, corrs, emit)


def assemble_kernel(n_seg, params, near_ref, *refs):
    groups, (out_ref, mean, sems) = refs[:-3], refs[-3:]
    half = out_ref.shape[1] // 2
    part = params[2 * TX + 1] % 2

    def total(values):
        return functools.reduce(jnp.add, [v.astype(jnp.float32) for v in values]) * (1.0 / n_seg)

    copies = []
    for g in range(2):
        own, *arrived = groups[g * (n_seg - 1) : (g + 1) * (n_seg - 1)]
        for k in range(HALF_TX):
            at = g * HALF_TX + k
            mean[at, pl.ds(part * half, half)] = total([r[k] for r in (own, *arrived[0::2])])
            theirs = total([near_ref[at]] + [r[k] for r in arrived[1::2]])
            mean[at, pl.ds((1 - part) * half, half)] = theirs
            copy = pltpu.make_async_copy(
                mean.at[at], out_ref.at[first_tx(params, g) + k], sems.at[at]
            )
            copy.start()
            copies.append(copy)
    for copy in copies:
        copy.wait()


def call_powers(kernel, name, args, out_shape, count, segments, flops):
    return pl.pallas_call(
        kernel,
        in_specs=[SMEM if a.ndim == 1 else VMEM for a in args],
        out_specs=[VMEM] * len(out_shape),
        out_shape=out_shape,
        scratch_shapes=[pltpu.VMEM((BLOCKS + 2 * PAD, PAIR), jnp.float32)]
        + [pltpu.VMEM((HALF_TX, 2 * FFT, BLOCKS), jnp.float32)] * segments
        + [
            pltpu.VMEM((segments, 2 * FFT, count * BLOCKS), jnp.bfloat16),
            pltpu.VMEM((HALF_TX, segments * count * DELAYS, 2 * BLOCKS), jnp.bfloat16),
        ],
        compiler_params=pltpu.CompilerParams(vmem_limit_bytes=VMEM_LIMIT * count // 8),
        cost_estimate=pl.CostEstimate(flops=flops, bytes_accessed=1 << 20, transcendentals=0),
        name=name,
    )(*args)


def swap(value, axis, flip):
    size = lax.axis_size(axis)
    return lax.ppermute(value, axis, [(i, i ^ flip) for i in range(size)])


def shards(voltages, surv_taps, ref_taps, tx_owner, delay_start, doppler_start):
    beams_here = voltages.shape[1]
    n_beam = lax.axis_size("beam")
    n_seg = lax.axis_size("seg")
    ids = jnp.stack([lax.axis_index("beam"), lax.axis_index("seg")]).astype(jnp.int32)
    volts = voltages.reshape(2, beams_here, voltages.shape[3])
    out = decimate(
        volts,
        surv_taps.reshape(1, TAPS),
        ref_taps.reshape(1, TAPS),
        ids,
        tx_owner,
        delay_start,
        doppler_start,
    )
    here, give, keep, send, params = out
    stab, rtab = jnp.asarray(surv_fourier()), jnp.asarray(ref_fourier())
    there = swap(give, "seg", 1)
    half = keep + swap(send, "beam", 1)
    half, here, params = lax.optimization_barrier((half, here, params))
    got = [swap(half, "beam", flip) for flip in range(2, n_beam, 2)]
    lags, dops = make_tables(params, n_seg)
    spec = surv_spectra(stab, here, "own_spectra")
    got, lags, dops, spec = lax.optimization_barrier((got, lags, dops, spec))
    half = functools.reduce(jnp.add, got, half)
    other = swap(half, "beam", 1)
    far = swap(half, "seg", 1)
    far_other = swap(other, "seg", 1)
    count = beams_here // 2
    each = DELAYS // n_seg
    kept = lambda n: jax.ShapeDtypeStruct((HALF_TX, count, n, DOPPLER), jnp.float32)
    sent = lambda n: jax.ShapeDtypeStruct((n, count, each, DOPPLER), jnp.bfloat16)
    (part,) = call_powers(
        own_part_kernel,
        "own_part",
        (params, rtab, half, spec, lags, dops),
        [kept(DELAYS)],
        count,
        1,
        OWN_FLOPS,
    )
    part, there = lax.optimization_barrier((part, there))
    far_spec, own, near, *long_way = call_powers(
        far_part_kernel,
        "far_part",
        (params, rtab, far, stab, there, part, lags, dops),
        [jax.ShapeDtypeStruct(spec.shape, spec.dtype), kept(each)] + [sent(HALF_TX)] * (n_seg - 1),
        count,
        1,
        FAR_FLOPS,
    )
    arrived = [swap(s, "seg", n) for n, s in enumerate(long_way, 2)]
    collected = [own] + arrived
    own, near, *long_way = call_powers(
        both_kernel,
        "both",
        (params, rtab, other, far_other, spec, far_spec, near, lags, dops),
        [kept(each), sent(TX)] + [sent(HALF_TX)] * (n_seg - 2),
        count,
        2,
        BOTH_FLOPS,
    )
    near = swap(near, "seg", 1)
    long_way[0], *arrived = lax.optimization_barrier((long_way[0], *arrived))
    collected += [own] + [swap(s, "seg", n) for n, s in enumerate(long_way, 2)]
    out = (TX, beams_here, each, DOPPLER)
    return pl.pallas_call(
        functools.partial(assemble_kernel, n_seg),
        in_specs=[SMEM] + [VMEM] * (1 + len(collected)),
        out_specs=pl.BlockSpec(memory_space=pl.ANY),
        out_shape=jax.ShapeDtypeStruct(out, jnp.float32),
        scratch_shapes=[pltpu.VMEM(out, jnp.float32), pltpu.SemaphoreType.DMA((TX,))],
        compiler_params=pltpu.CompilerParams(vmem_limit_bytes=VMEM_LIMIT),
        name="assemble",
    )(params, near, *collected)


def solution(mesh):
    return jax.shard_map(
        shards,
        mesh=mesh,
        in_specs=(P(None, "beam", "seg", None), P(), P(), P(), P(), P()),
        out_specs=P(None, "beam", "seg", None),
        check_vma=False,
    )
```
